32 devices in a mesh: rows: 4 (over y, x), feat: 8 (over z, core).
Axes of the slice: x: 2, y: 2, z: 4, core: 2. Of those that a mesh axis runs over, the one named last changes fastest.
Arguments:
- node_feats: bfloat16 [2048, 1024], P('rows', 'feat'), may hold values from -6 to 6
- weight: bfloat16 [1024, 1024], P(None, 'feat'), may hold values from -0.1875 to 0.1875
- root_weight: bfloat16 [1024, 1024], P(None, 'feat'), may hold values from -0.1875 to 0.1875
- grad_out: bfloat16 [2048, 1024], P('rows', 'feat'), may hold values from -6 to 6
- block_counts: int32 [16], P('rows'), may hold values from 1 to 40, as said below
- tile_cols: int32 [320], P('rows'), may hold values from 0 to 15
- tile_vals: bfloat16 [320, 128, 128], P('rows'), may hold values from -0.125 to 0.125
Outputs:
- grad_feats: bfloat16 [2048, 1024], P('rows', 'feat')
- grad_weight: float32 [1024, 1024], P(None, 'feat')
- grad_root: float32 [1024, 1024], P(None, 'feat')
The draws below stay inside these ranges and needn't reach their ends.
Inputs may be any that keep to these rules, and one draw needn't show every extreme that they name: `block_counts`: the counts of the 4 row blocks of one index of rows sum to at most 80; in every draw one index of rows fills all its 80 slots and one of its blocks has 40 tiles.
All inputs are finite; a program needn't handle non-finite values.
Results may differ from the reference program's by a relative error of at most 0.0059.
Values may be sent and summed in bfloat16 or wider, within the bound.
No kernel may reach another device: no remote copies, remote signals or barrier semaphores. Data moves between devices by JAX's collectives and lax.ppermute only.
A program may use at most 64 MiB of HBM per device.

```python
import jax
import jax.numpy as jnp
from jax import lax

F = 1024
TILE = 128
NB_DEV = 4
MOST = 40
TILE_CAP = 80
NBLK = 16
NODES = 2048
TILES = 320


def draw_block_counts(key, part):
    nrows = NBLK // NB_DEV
    light = jax.random.randint(jax.random.fold_in(key, 11), (nrows, NB_DEV), 1, 21)
    heavy = jax.random.randint(jax.random.fold_in(key, 12), (), 0, nrows)
    order = jax.random.permutation(jax.random.fold_in(key, 13), NB_DEV)
    places = jnp.arange(NB_DEV, dtype=jnp.int32)
    pattern = jnp.full((NB_DEV,), 20, jnp.int32)
    pattern = jnp.where(places == order[0], MOST, pattern)
    pattern = jnp.where(places == order[1], 19, pattern)
    pattern = jnp.where(places == order[2], 1, pattern)
    counts = jnp.where(jnp.arange(nrows, dtype=jnp.int32)[:, None] == heavy, pattern[None, :], light)
    return counts.reshape(-1).astype(jnp.int32)


def touch_ends(array, key, low, largest):
    place = [jax.random.randint(jax.random.fold_in(key, axis), (), 0, length) for axis, length in enumerate(array.shape)]
    widest = array.shape.index(max(array.shape))
    next_to = place[:widest] + [(place[widest] + 1) % array.shape[widest]] + place[widest + 1:]
    return array.at[tuple(place)].set(low).at[tuple(next_to)].set(largest)


def block_scale(rng, shape, split, least, largest):
    loudness, own = 1.0, jax.random.fold_in(rng, 6)
    for axis_at, blocks in split:
        steps = jnp.exp(jax.random.uniform(jax.random.fold_in(own, axis_at), (blocks,), jnp.float32, least / len(split), largest / len(split)))
        loudness = loudness * jnp.repeat(steps, shape[axis_at] // blocks).reshape([-1 if axis == axis_at else 1 for axis in range(len(shape))])
    return loudness


def centred(key, shape, deviation, most, pieces=(), kind=jnp.bfloat16):
    result = deviation * jax.random.normal(key, shape, jnp.float32)
    if pieces:
        result = result * block_scale(key, shape, pieces, -0.22, 0.18)
    return jnp.clip(result, -most, most).astype(kind)


def setup_inputs(seed: int = 0) -> dict:
    splits = jax.random.split(jax.random.key(seed), 8)
    node_feats = centred(splits[0], (NODES, F), 1.0, 6.0, ((0, 4), (1, 8)))
    weight = centred(splits[1], (F, F), F ** -0.5, 0.1875, ((1, 8),))
    root_weight = centred(splits[2], (F, F), F ** -0.5, 0.1875, ((1, 8),))
    grad_out = centred(splits[3], (NODES, F), 1.0, 6.0, ((0, 4), (1, 8)))
    block_counts = draw_block_counts(jax.random.fold_in(splits[7], 71), 0)
    tile_cols = touch_ends(jax.random.randint(splits[5], (TILES,), 0, NBLK), jax.random.fold_in(splits[5], 1), 0, NBLK - 1).astype(jnp.int32)
    tile_vals = centred(splits[6], (TILES, TILE, TILE), (TILE * 16) ** -0.5, 0.125, ((0, 4),))
    return dict(node_feats=node_feats, weight=weight, root_weight=root_weight, grad_out=grad_out, block_counts=block_counts, tile_cols=tile_cols, tile_vals=tile_vals)


def reference(node_feats, weight, root_weight, grad_out, block_counts, tile_cols, tile_vals):
    hidden = jnp.dot(node_feats, weight, preferred_element_type=jnp.float32).astype(jnp.bfloat16)
    own = jnp.dot(node_feats, root_weight, preferred_element_type=jnp.float32)
    nrows = NBLK // NB_DEV
    counts = block_counts.reshape(nrows, NB_DEV)
    cols = tile_cols.reshape(nrows, TILE_CAP)
    values = tile_vals.reshape(nrows, TILE_CAP, TILE, TILE)
    hblocks = hidden.reshape(NBLK, TILE, F)
    slots = jnp.arange(TILE_CAP, dtype=jnp.int32)

    def owners(cnt):
        ends = jnp.cumsum(cnt)
        return jnp.sum((ends[None, :] <= slots[:, None]).astype(jnp.int32), axis=1).astype(jnp.int32)

    def forward_one(args):
        cnt, col, val = args
        owner = owners(cnt)
        prod = jnp.einsum("tij,tjf->tif", val.astype(jnp.float32), hblocks[col].astype(jnp.float32))
        return jax.ops.segment_sum(prod, owner, num_segments=NB_DEV + 1)[:NB_DEV]

    agg = lax.map(forward_one, (counts, cols, values))
    pre = agg.reshape(NODES, F) + own
    sig = jax.nn.sigmoid(pre)
    grad_pre = (grad_out.astype(jnp.float32) * sig * (1.0 + pre * (1.0 - sig))).astype(jnp.bfloat16)
    dblocks = grad_pre.reshape(nrows, NB_DEV, TILE, F)

    def backward_one(acc, args):
        cnt, col, val, dzb = args
        owner = owners(cnt)
        live = (owner < NB_DEV).astype(jnp.float32)
        src = dzb[jnp.minimum(owner, NB_DEV - 1)].astype(jnp.float32)
        contrib = jnp.einsum("tij,tif->tjf", val.astype(jnp.float32), src) * live[:, None, None]
        return acc + jax.ops.segment_sum(contrib, col, num_segments=NBLK), None

    grad_sum, unused = lax.scan(backward_one, jnp.zeros((NBLK, TILE, F), jnp.float32), (counts, cols, values, dblocks))
    grad_hidden = grad_sum.reshape(NODES, F).astype(jnp.bfloat16)
    grad_weight = jnp.dot(node_feats.T, grad_hidden, preferred_element_type=jnp.float32)
    grad_root = jnp.dot(node_feats.T, grad_pre, preferred_element_type=jnp.float32)
    grad_feats = (jnp.dot(grad_hidden, weight.T, preferred_element_type=jnp.float32) + jnp.dot(grad_pre, root_weight.T, preferred_element_type=jnp.float32)).astype(jnp.bfloat16)
    return (grad_feats, grad_weight, grad_root)
```

```python
import functools

import jax
import jax.numpy as jnp
from jax import lax
from jax.experimental import pallas as pl
from jax.experimental.pallas import tpu as pltpu
from jax.sharding import PartitionSpec as P

BF = jnp.bfloat16
F32 = jnp.float32
VMEM = pl.BlockSpec(memory_space=pltpu.VMEM)
SMEM = pl.BlockSpec(memory_space=pltpu.SMEM)


def dot(a, b):
    return jnp.dot(a, b, preferred_element_type=F32)


def dot_nt(a, b):
    return lax.dot_general(a, b, (((1,), (1,)), ((), ())), preferred_element_type=F32)


def call(body, outs, specs, args, flops=0, scratch=(), limit=None):
    moved = sum(a.size * a.dtype.itemsize for a in args)
    moved += sum(o.size * o.dtype.itemsize for o in outs)
    return pl.pallas_call(
        body,
        out_shape=outs,
        in_specs=specs,
        out_specs=[VMEM] * len(outs),
        scratch_shapes=scratch,
        compiler_params=pltpu.CompilerParams(vmem_limit_bytes=limit or 32 * 1024 * 1024),
        cost_estimate=pl.CostEstimate(flops=flops, bytes_accessed=moved, transcendentals=0),
    )(*args)


def sds(shape, dtype):
    return jax.ShapeDtypeStruct(shape, dtype)


def assemble_kernel(counts, cols, vals, adj, adj_t, acc):
    nblocks = counts.shape[0]
    tile = vals.shape[1]
    all_blocks = adj.shape[1] // tile
    acc[...] = jnp.zeros_like(acc)
    start = jnp.int32(0)
    for b in range(nblocks):
        rows = slice(b * tile, (b + 1) * tile)

        def add(t, carry, rows=rows):
            place = pl.ds(pl.multiple_of(cols[t] * tile, tile), tile)
            acc[rows, place] += vals[t].astype(F32)
            return carry

        end = start + counts[b]
        lax.fori_loop(start, end, add, 0)
        start = end

    def finish(c, carry):
        place = pl.ds(pl.multiple_of(c * tile, tile), tile)
        block = acc[:, place]
        adj[:, place] = block.astype(BF)
        adj_t[place, :] = block.T.astype(BF)
        return carry

    lax.fori_loop(0, all_blocks, finish, 0)


def forward_kernel(nf, *refs):
    pieces, (weight, root, hidden, own) = refs[:nf], refs[nf:]
    me = lax.axis_index("feat")
    width = weight.shape[1]
    total = None
    for k in range(nf // 2):
        even = pl.ds(pl.multiple_of((me ^ (2 * k)) * width, width), width)
        odd = pl.ds(pl.multiple_of((me ^ (2 * k + 1)) * width, width), width)
        left = jnp.concatenate([pieces[2 * k][...], pieces[2 * k + 1][...]], 1)
        right = jnp.concatenate(
            [
                jnp.concatenate([weight[even, :], root[even, :]], 1),
                jnp.concatenate([weight[odd, :], root[odd, :]], 1),
            ],
            0,
        )
        part = dot(left, right)
        total = part if total is None else total + part
    hidden[...] = total[:, :width].astype(BF)
    own[...] = total[:, width:]


def transpose_kernel(nf, *refs):
    pieces, out = refs[:nf], refs[nf]
    me = lax.axis_index("feat")
    width = pieces[0].shape[1]
    for m in range(nf):
        rows = pl.ds(pl.multiple_of((me ^ m) * width, width), width)
        out[rows, :] = pieces[m][...].T


def aggregate_kernel(nr, *refs):
    hidden = refs[:nr]
    adj, adj_t, own, grad_out, grad_pre, kept = refs[nr : nr + 6]
    sent = refs[nr + 6 :]
    me = lax.axis_index("rows")
    rows = own.shape[0]
    pre = own[...]
    for j in range(nr):
        place = pl.ds(pl.multiple_of((me ^ j) * rows, rows), rows)
        pre = pre + dot(adj[:, place], hidden[j][...])
    sig = jax.nn.sigmoid(pre)
    grad = (grad_out[...].astype(F32) * sig * (1.0 + pre * (1.0 - sig))).astype(BF)
    grad_pre[...] = grad
    for j in range(nr):
        place = pl.ds(pl.multiple_of((me ^ j) * rows, rows), rows)
        part = dot(adj_t[place, :], grad)
        if j == 0:
            kept[...] = part
        else:
            sent[j - 1][...] = part.astype(BF)


def sum_kernel(n, *refs):
    total = refs[0][...].astype(F32)
    for ref in refs[1:n]:
        total = total + ref[...].astype(F32)
    refs[n][...] = total.astype(refs[n].dtype)


def feats_kernel(nz, hidden, pre, hidden_2, pre_2, weight, root, weight_2, root_2, kept, *sent):
    me = lax.axis_index("feat")
    width = weight.shape[1]
    left = jnp.concatenate([hidden[...], pre[...], hidden_2[...], pre_2[...]], 1)
    for k in range(nz):
        rows = pl.ds(pl.multiple_of((me ^ (2 * k)) * width, width), width)
        right = jnp.concatenate(
            [weight[rows, :], root[rows, :], weight_2[rows, :], root_2[rows, :]], 1
        )
        part = dot_nt(left, right)
        if k == 0:
            kept[...] = part
        else:
            sent[k - 1][...] = part.astype(BF)


def weights_kernel(nr, feats_t, hidden, pre, kept, *rest):
    sent, whole = rest[:-1], rest[-1]
    me = lax.axis_index("rows")
    share = kept.shape[0]
    whole[...] = dot(feats_t[...], jnp.concatenate([hidden[...], pre[...]], 1))
    for j in range(nr):
        part = whole[pl.ds(pl.multiple_of((me ^ j) * share, share), share), :]
        if j == 0:
            kept[...] = part
        else:
            sent[j - 1][...] = part.astype(BF)


def place_kernel(nr, *refs):
    pieces, (weight, root) = refs[:nr], refs[nr:]
    me = lax.axis_index("rows")
    share, width = pieces[0].shape[0], weight.shape[1]
    for j in range(nr):
        rows = pl.ds(pl.multiple_of((me ^ j) * share, share), share)
        block = pieces[j][...].astype(F32)
        weight[rows, :] = block[:, :width]
        root[rows, :] = block[:, width:]


def on_device(node_feats, weight, root_weight, grad_out, block_counts, tile_cols, tile_vals):
    rows, width = node_feats.shape
    depth = weight.shape[0]
    nr, nf = lax.axis_size("rows"), lax.axis_size("feat")
    nz = nf // 2
    nodes = rows * nr
    share = depth // nr

    def swap(array, axis, mask):
        return lax.ppermute(array, axis, [(i, i ^ mask) for i in range(lax.axis_size(axis))])

    mine = [node_feats] + [swap(node_feats, "feat", 2 * k) for k in range(1, nz)]
    pieces = []
    for piece in mine:
        pieces += [piece, swap(piece, "feat", 1)]
    weight_2, root_2 = swap(weight, "feat", 1), swap(root_weight, "feat", 1)

    adj, adj_t = call(
        assemble_kernel,
        [sds((rows, nodes), BF), sds((nodes, rows), BF)],
        [SMEM, SMEM, VMEM],
        (block_counts, tile_cols, tile_vals),
        flops=4 * rows * nodes,
        scratch=[pltpu.VMEM((rows, nodes), F32)],
        limit=16 * rows * nodes,
    )
    hidden, own = call(
        functools.partial(forward_kernel, nf),
        [sds((rows, width), BF), sds((rows, width), F32)],
        [VMEM] * (nf + 2),
        (*pieces, weight, root_weight),
        flops=4 * rows * depth * width,
    )
    gathered = [hidden] + [swap(hidden, "rows", j) for j in range(1, nr)]
    (feats_t,) = call(
        functools.partial(transpose_kernel, nf),
        [sds((depth, rows), BF)],
        [VMEM] * nf,
        pieces,
    )
    grad_pre, kept, *sent = call(
        functools.partial(aggregate_kernel, nr),
        [sds((rows, width), BF), sds((rows, width), F32)] + [sds((rows, width), BF)] * (nr - 1),
        [VMEM] * (nr + 4),
        (*gathered, adj, adj_t, own, grad_out),
        flops=4 * rows * nodes * width,
        limit=max(32 * 1024 * 1024, 10 * rows * nodes),
    )
    pre_2 = swap(grad_pre, "feat", 1)
    sums = [kept] + [swap(part, "rows", j + 1) for j, part in enumerate(sent)]
    (grad_hidden,) = call(
        functools.partial(sum_kernel, nr), [sds((rows, width), BF)], [VMEM] * nr, sums
    )
    hidden_2 = swap(grad_hidden, "feat", 1)
    kept_w, *sent_w = call(
        functools.partial(weights_kernel, nr),
        [sds((share, 2 * width), F32)] + [sds((share, 2 * width), BF)] * (nr - 1),
        [VMEM] * 3,
        (feats_t, grad_hidden, grad_pre),
        flops=4 * rows * depth * width,
        scratch=[pltpu.VMEM((depth, 2 * width), F32)],
    )
    kept_f, *sent_f = call(
        functools.partial(feats_kernel, nz),
        [sds((rows, width), F32)] + [sds((rows, width), BF)] * (nz - 1),
        [VMEM] * 8,
        (grad_hidden, grad_pre, hidden_2, pre_2, weight, root_weight, weight_2, root_2),
        flops=4 * rows * depth * width,
    )
    sums_f = [kept_f] + [swap(part, "feat", 2 * (k + 1)) for k, part in enumerate(sent_f)]
    sums_w = [kept_w] + [swap(part, "rows", j + 1) for j, part in enumerate(sent_w)]
    (shared,) = call(
        functools.partial(sum_kernel, nr), [sds((share, 2 * width), BF)], [VMEM] * nr, sums_w
    )
    all_shared = [shared] + [swap(shared, "rows", j) for j in range(1, nr)]
    grad_weight, grad_root = call(
        functools.partial(place_kernel, nr),
        [sds((depth, width), F32)] * 2,
        [VMEM] * nr,
        all_shared,
    )
    (grad_feats,) = call(
        functools.partial(sum_kernel, nz), [sds((rows, width), BF)], [VMEM] * nz, sums_f
    )
    return grad_feats, grad_weight, grad_root


def solution(mesh):
    placed = (
        P("rows", "feat"),
        P(None, "feat"),
        P(None, "feat"),
        P("rows", "feat"),
        P("rows"),
        P("rows"),
        P("rows", None, None),
    )
    return jax.shard_map(
        on_device,
        mesh=mesh,
        in_specs=placed,
        out_specs=(P("rows", "feat"), P(None, "feat"), P(None, "feat")),
        check_vma=False,
    )
```

```python
import functools

import jax
import jax.numpy as jnp
from jax import lax
from jax.experimental import pallas as pl
from jax.experimental.pallas import tpu as pltpu
from jax.sharding import PartitionSpec as P

BF = jnp.bfloat16
F32 = jnp.float32
VMEM = pl.BlockSpec(memory_space=pltpu.VMEM)
SMEM = pl.BlockSpec(memory_space=pltpu.SMEM)
ANY = pl.BlockSpec(memory_space=pl.ANY)


def dot(a, b):
    return jnp.dot(a, b, preferred_element_type=F32)


def dot_nt(a, b):
    return lax.dot_general(a, b, (((1,), (1,)), ((), ())), preferred_element_type=F32)


def call(body, outs, specs, args, flops=0, scratch=(), limit=None):
    moved = sum(a.size * a.dtype.itemsize for a in args)
    moved += sum(o.size * o.dtype.itemsize for o in outs)
    return pl.pallas_call(
        body,
        out_shape=outs,
        in_specs=specs,
        out_specs=[VMEM] * len(outs),
        scratch_shapes=scratch,
        compiler_params=pltpu.CompilerParams(vmem_limit_bytes=limit or 32 * 1024 * 1024),
        cost_estimate=pl.CostEstimate(flops=flops, bytes_accessed=moved, transcendentals=0),
    )(*args)


def sds(shape, dtype):
    return jax.ShapeDtypeStruct(shape, dtype)


def prepare_kernel(
    nf, counts, cols, vals, feats, weight, root, adj, adj_t, mine, near, far, tiles, acc, sems
):
    nblocks = counts.shape[0]
    tile = vals.shape[1]
    all_blocks = adj.shape[1] // tile
    width = weight.shape[1]
    me = lax.axis_index("feat")
    copies = [pltpu.make_async_copy(vals, tiles, sems.at[0])]
    copies.append(pltpu.make_async_copy(feats, mine, sems.at[1]))
    for k in range(nf // 2):
        for flip, out in ((0, near), (1, far)):
            rows = pl.ds(pl.multiple_of((me ^ (2 * k + flip)) * width, width), width)
            for half, array in enumerate((weight, root)):
                place = out.at[half, k * width : (k + 1) * width, :]
                copies.append(pltpu.make_async_copy(array.at[rows, :], place, sems.at[len(copies)]))
    for copy in copies:
        copy.start()
    acc[...] = jnp.zeros_like(acc)
    copies[0].wait()
    start = jnp.int32(0)
    for b in range(nblocks):
        rows = slice(b * tile, (b + 1) * tile)

        def add(t, carry, rows=rows):
            place = pl.ds(pl.multiple_of(cols[t] * tile, tile), tile)
            acc[rows, place] += tiles[t].astype(F32)
            return carry

        end = start + counts[b]
        lax.fori_loop(start, end, add, 0)
        start = end

    def finish(c, carry):
        place = pl.ds(pl.multiple_of(c * tile, tile), tile)
        block = acc[:, place]
        adj[:, place] = block.astype(BF)
        adj_t[place, :] = block.T.astype(BF)
        return carry

    lax.fori_loop(0, all_blocks, finish, 0)
    for copy in copies[1:]:
        copy.wait()


def forward_kernel(nf, *refs):
    pieces, (near, far, hidden, own) = refs[:nf], refs[nf:]
    width = hidden.shape[1]
    total = None
    for k in range(nf // 2):
        place = slice(k * width, (k + 1) * width)
        left = jnp.concatenate([pieces[2 * k][...], pieces[2 * k + 1][...]], 1)
        top = jnp.concatenate([near[0, place, :], near[1, place, :]], 1)
        bottom = jnp.concatenate([far[0, place, :], far[1, place, :]], 1)
        part = dot(left, jnp.concatenate([top, bottom], 0))
        total = part if total is None else total + part
    hidden[...] = total[:, :width].astype(BF)
    own[...] = total[:, width:]


def transpose_kernel(nf, *refs):
    pieces, out = refs[:nf], refs[nf]
    me = lax.axis_index("feat")
    width = pieces[0].shape[1]
    for m in range(nf):
        rows = pl.ds(pl.multiple_of((me ^ m) * width, width), width)
        out[rows, :] = pieces[m][...].T


def aggregate_kernel(nr, *refs):
    hidden = refs[:nr]
    adj, adj_t, own, grad_out, grad_pre, kept = refs[nr : nr + 6]
    sent = refs[nr + 6 :]
    me = lax.axis_index("rows")
    rows = own.shape[0]
    pre = own[...]
    for j in range(nr):
        place = pl.ds(pl.multiple_of((me ^ j) * rows, rows), rows)
        pre = pre + dot(adj[:, place], hidden[j][...])
    sig = jax.nn.sigmoid(pre)
    grad = (grad_out[...].astype(F32) * sig * (1.0 + pre * (1.0 - sig))).astype(BF)
    grad_pre[...] = grad
    for j in range(nr):
        place = pl.ds(pl.multiple_of((me ^ j) * rows, rows), rows)
        part = dot(adj_t[place, :], grad)
        if j == 0:
            kept[...] = part
        else:
            sent[j - 1][...] = part.astype(BF)


def sum_kernel(n, *refs):
    total = refs[0][...].astype(F32)
    for ref in refs[1:n]:
        total = total + ref[...].astype(F32)
    refs[n][...] = total.astype(refs[n].dtype)


def feats_kernel(nz, hidden, pre, hidden_2, pre_2, near, near_2, kept, *sent):
    width = hidden.shape[1]
    left = jnp.concatenate([hidden[...], pre[...], hidden_2[...], pre_2[...]], 1)
    for k in range(nz):
        place = slice(k * width, (k + 1) * width)
        right = [near[0, place, :], near[1, place, :], near_2[0, place, :], near_2[1, place, :]]
        part = dot_nt(left, jnp.concatenate(right, 1))
        if k == 0:
            kept[...] = part
        else:
            sent[k - 1][...] = part.astype(BF)


def weights_kernel(nr, feats_t, hidden, pre, after, kept, *rest):
    sent, whole = rest[:-1], rest[-1]
    me = lax.axis_index("rows")
    share = kept.shape[0]
    whole[...] = dot(feats_t[...], jnp.concatenate([hidden[...], pre[...]], 1))
    for j in range(nr):
        part = whole[pl.ds(pl.multiple_of((me ^ j) * share, share), share), :]
        if j == 0:
            kept[...] = part
        else:
            sent[j - 1][...] = part.astype(BF)


def place_kernel(nr, *refs):
    pieces, (weight, root) = refs[:nr], refs[nr:]
    me = lax.axis_index("rows")
    share, width = pieces[0].shape[0], weight.shape[1]
    for j in range(nr):
        rows = pl.ds(pl.multiple_of((me ^ j) * share, share), share)
        block = pieces[j][...].astype(F32)
        weight[rows, :] = block[:, :width]
        root[rows, :] = block[:, width:]


def on_device(node_feats, weight, root_weight, grad_out, block_counts, tile_cols, tile_vals):
    rows, width = node_feats.shape
    depth = weight.shape[0]
    nr, nf = lax.axis_size("rows"), lax.axis_size("feat")
    nz = nf // 2
    nodes = rows * nr
    share = depth // nr

    def swap(array, axis, mask):
        return lax.ppermute(array, axis, [(i, i ^ mask) for i in range(lax.axis_size(axis))])

    moved = [node_feats] + [swap(node_feats, "feat", 2 * k) for k in range(1, nz)]
    adj, adj_t, mine, near, far = call(
        functools.partial(prepare_kernel, nf),
        [
            sds((rows, nodes), BF),
            sds((nodes, rows), BF),
            sds((rows, width), BF),
            sds((2, depth // 2, width), BF),
            sds((2, depth // 2, width), BF),
        ],
        [SMEM, SMEM] + [ANY] * 4,
        (block_counts, tile_cols, tile_vals, node_feats, weight, root_weight),
        flops=4 * rows * nodes,
        scratch=[
            pltpu.VMEM(tile_vals.shape, BF),
            pltpu.VMEM((rows, nodes), F32),
            pltpu.SemaphoreType.DMA((2 + 2 * nf,)),
        ],
        limit=18 * rows * nodes,
    )
    arrived = lax.optimization_barrier((mine, *moved[1:], near))[:-1]
    pieces = []
    for piece in arrived:
        pieces += [piece, swap(piece, "feat", 1)]
    near_2 = swap(far, "feat", 1)
    hidden, own = call(
        functools.partial(forward_kernel, nf),
        [sds((rows, width), BF), sds((rows, width), F32)],
        [VMEM] * (nf + 2),
        (*pieces, near, far),
        flops=4 * rows * depth * width,
    )
    gathered = [hidden] + [swap(hidden, "rows", j) for j in range(1, nr)]
    (feats_t,) = call(
        functools.partial(transpose_kernel, nf),
        [sds((depth, rows), BF)],
        [VMEM] * nf,
        pieces,
    )
    grad_pre, kept, *sent = call(
        functools.partial(aggregate_kernel, nr),
        [sds((rows, width), BF), sds((rows, width), F32)] + [sds((rows, width), BF)] * (nr - 1),
        [VMEM] * (nr + 4),
        (*gathered, adj, adj_t, own, grad_out),
        flops=4 * rows * nodes * width,
        limit=max(32 * 1024 * 1024, 10 * rows * nodes),
    )
    pre_2 = swap(grad_pre, "feat", 1)
    sums = [kept] + [swap(part, "rows", j + 1) for j, part in enumerate(sent)]
    (grad_hidden,) = call(
        functools.partial(sum_kernel, nr), [sds((rows, width), BF)], [VMEM] * nr, sums
    )
    hidden_2 = swap(grad_hidden, "feat", 1)
    kept_f, *sent_f = call(
        functools.partial(feats_kernel, nz),
        [sds((rows, width), F32)] + [sds((rows, width), BF)] * (nz - 1),
        [VMEM] * 6,
        (grad_hidden, grad_pre, hidden_2, pre_2, near, near_2),
        flops=4 * rows * depth * width,
    )
    kept_w, *sent_w = call(
        functools.partial(weights_kernel, nr),
        [sds((share, 2 * width), F32)] + [sds((share, 2 * width), BF)] * (nr - 1),
        [VMEM] * 3 + [ANY],
        (feats_t, grad_hidden, grad_pre, kept_f),
        flops=4 * rows * depth * width,
        scratch=[pltpu.VMEM((depth, 2 * width), F32)],
    )
    sums_f = [kept_f] + [swap(part, "feat", 2 * (k + 1)) for k, part in enumerate(sent_f)]
    sums_w = [kept_w] + [swap(part, "rows", j + 1) for j, part in enumerate(sent_w)]
    (shared,) = call(
        functools.partial(sum_kernel, nr), [sds((share, 2 * width), BF)], [VMEM] * nr, sums_w
    )
    all_shared = [shared] + [swap(shared, "rows", j) for j in range(1, nr)]
    grad_weight, grad_root = call(
        functools.partial(place_kernel, nr),
        [sds((depth, width), F32)] * 2,
        [VMEM] * nr,
        all_shared,
    )
    (grad_feats,) = call(
        functools.partial(sum_kernel, nz), [sds((rows, width), BF)], [VMEM] * nz, sums_f
    )
    return grad_feats, grad_weight, grad_root


def solution(mesh):
    placed = (
        P("rows", "feat"),
        P(None, "feat"),
        P(None, "feat"),
        P("rows", "feat"),
        P("rows"),
        P("rows"),
        P("rows", None, None),
    )
    return jax.shard_map(
        on_device,
        mesh=mesh,
        in_specs=placed,
        out_specs=(P("rows", "feat"), P(None, "feat"), P(None, "feat")),
        check_vma=False,
    )
```

```python
import functools

import jax
import jax.numpy as jnp
from jax import lax
from jax.experimental import pallas as pl
from jax.experimental.pallas import tpu as pltpu
from jax.sharding import PartitionSpec as P

BF = jnp.bfloat16
F32 = jnp.float32
VMEM = pl.BlockSpec(memory_space=pltpu.VMEM)
SMEM = pl.BlockSpec(memory_space=pltpu.SMEM)
HBM = pl.BlockSpec(memory_space=pltpu.HBM)


def dot(a, b):
    return jnp.dot(a, b, preferred_element_type=F32)


def dot_nt(a, b):
    return lax.dot_general(a, b, (((1,), (1,)), ((), ())), preferred_element_type=F32)


def call(body, outs, specs, args, flops=0, scratch=(), limit=None):
    moved = sum(a.size * a.dtype.itemsize for a in args)
    moved += sum(o.size * o.dtype.itemsize for o in outs)
    return pl.pallas_call(
        body,
        out_shape=outs,
        in_specs=specs,
        out_specs=[VMEM] * len(outs),
        scratch_shapes=scratch,
        compiler_params=pltpu.CompilerParams(vmem_limit_bytes=limit or 32 * 1024 * 1024),
        cost_estimate=pl.CostEstimate(flops=flops, bytes_accessed=moved, transcendentals=0),
    )(*args)


def sds(shape, dtype):
    return jax.ShapeDtypeStruct(shape, dtype)


def assemble_kernel(all_counts, all_cols, vals, adj, counts, cols, tiles, acc, sems):
    nblocks = counts.shape[0]
    tile = vals.shape[1]
    pairs = ((all_counts, counts), (all_cols, cols), (vals, tiles))
    copies = [pltpu.make_async_copy(*pair, sems.at[i]) for i, pair in enumerate(pairs)]
    for copy in copies:
        copy.start()
    acc[...] = jnp.zeros_like(acc)
    for copy in copies:
        copy.wait()
    start = jnp.int32(0)
    for b in range(nblocks):
        rows = slice(b * tile, (b + 1) * tile)

        def add(t, carry, rows=rows):
            place = pl.ds(pl.multiple_of(cols[t] * tile, tile), tile)
            acc[rows, place] += tiles[t].astype(F32)
            return carry

        end = start + counts[b]
        lax.fori_loop(start, end, add, 0)
        start = end
    adj[...] = acc[...].astype(BF)


def flip_kernel(tile, adj, adj_t):
    def flip(c, carry):
        place = pl.ds(pl.multiple_of(c * tile, tile), tile)
        adj_t[place, :] = adj[:, place].T
        return carry

    lax.fori_loop(0, adj.shape[1] // tile, flip, 0)


def prepare_kernel(nf, feats, weight, root, mine, near, far):
    width = weight.shape[1]
    me = lax.axis_index("feat")
    mine[...] = feats[...]
    for k in range(nf // 2):
        place = slice(k * width, (k + 1) * width)
        for flip, out in ((0, near), (1, far)):
            rows = pl.ds(pl.multiple_of((me ^ (2 * k + flip)) * width, width), width)
            out[0, place, :] = weight[rows, :]
            out[1, place, :] = root[rows, :]


def forward_kernel(nf, *refs):
    pieces, (near, far, hidden, own) = refs[:nf], refs[nf:]
    width = hidden.shape[1]
    total = None
    for k in range(nf // 2):
        place = slice(k * width, (k + 1) * width)
        left = jnp.concatenate([pieces[2 * k][...], pieces[2 * k + 1][...]], 1)
        top = jnp.concatenate([near[0, place, :], near[1, place, :]], 1)
        bottom = jnp.concatenate([far[0, place, :], far[1, place, :]], 1)
        part = dot(left, jnp.concatenate([top, bottom], 0))
        total = part if total is None else total + part
    hidden[...] = total[:, :width].astype(BF)
    own[...] = total[:, width:]


def transpose_kernel(nf, *refs):
    pieces, out = refs[:nf], refs[nf]
    me = lax.axis_index("feat")
    width = pieces[0].shape[1]
    for m in range(nf):
        rows = pl.ds(pl.multiple_of((me ^ m) * width, width), width)
        out[rows, :] = pieces[m][...].T


def aggregate_kernel(nr, *refs):
    hidden = refs[:nr]
    adj, adj_t, own, grad_out, grad_pre, kept = refs[nr : nr + 6]
    sent = refs[nr + 6 :]
    me = lax.axis_index("rows")
    rows = own.shape[0]
    pre = own[...]
    for j in range(nr):
        place = pl.ds(pl.multiple_of((me ^ j) * rows, rows), rows)
        pre = pre + dot(adj[:, place], hidden[j][...])
    sig = jax.nn.sigmoid(pre)
    grad = (grad_out[...].astype(F32) * sig * (1.0 + pre * (1.0 - sig))).astype(BF)
    grad_pre[...] = grad
    for j in range(nr):
        place = pl.ds(pl.multiple_of((me ^ j) * rows, rows), rows)
        part = dot(adj_t[place, :], grad)
        if j == 0:
            kept[...] = part
        else:
            sent[j - 1][...] = part.astype(BF)


def sum_kernel(n, *refs):
    total = refs[0][...].astype(F32)
    for ref in refs[1:n]:
        total = total + ref[...].astype(F32)
    refs[n][...] = total.astype(refs[n].dtype)


def feats_kernel(nz, hidden, pre, hidden_2, pre_2, near, near_2, *out):
    width = hidden.shape[1]
    left = jnp.concatenate([hidden[...], pre[...], hidden_2[...], pre_2[...]], 1)
    for k in range(nz):
        place = slice(k * width, (k + 1) * width)
        right = [near[0, place, :], near[1, place, :], near_2[0, place, :], near_2[1, place, :]]
        out[k][...] = dot_nt(left, jnp.concatenate(right, 1)).astype(out[k].dtype)


def weights_kernel(feats_t, hidden, pre, weight, root):
    width = weight.shape[1]
    both = dot(feats_t[...], jnp.concatenate([hidden[...], pre[...]], 1))
    weight[...] = both[:, :width].astype(BF)
    root[...] = both[:, width:].astype(BF)


def pair_sum_kernel(weight, weight_2, root, root_2, weight_sum, root_sum):
    for out, terms in ((weight_sum, (weight, weight_2)), (root_sum, (root, root_2))):
        total = terms[0][...].astype(F32) + terms[1][...].astype(F32)
        out[...] = total.astype(out.dtype)


def on_device(node_feats, weight, root_weight, grad_out, block_counts, tile_cols, tile_vals):
    rows, width = node_feats.shape
    depth = weight.shape[0]
    nr, nf = lax.axis_size("rows"), lax.axis_size("feat")
    nz = nf // 2
    nodes = rows * nr

    def swap(array, axis, mask):
        return lax.ppermute(array, axis, [(i, i ^ mask) for i in range(lax.axis_size(axis))])

    (adj,) = call(
        assemble_kernel,
        [sds((rows, nodes), BF)],
        [HBM] * 3,
        (block_counts, tile_cols, tile_vals),
        flops=4 * rows * nodes,
        scratch=[
            pltpu.SMEM(block_counts.shape, jnp.int32),
            pltpu.SMEM(tile_cols.shape, jnp.int32),
            pltpu.VMEM(tile_vals.shape, BF),
            pltpu.VMEM((rows, nodes), F32),
            pltpu.SemaphoreType.DMA((3,)),
        ],
        limit=58 * 1024 * 1024,
    )
    mine, near, far = call(
        functools.partial(prepare_kernel, nf),
        [sds((rows, width), BF)] + [sds((2, depth // 2, width), BF)] * 2,
        [VMEM] * 3,
        (node_feats, weight, root_weight),
    )
    (adj_t,) = call(
        functools.partial(flip_kernel, tile_vals.shape[1]), [sds((nodes, rows), BF)], [VMEM], (adj,)
    )
    masks = [1 << bit for bit in range(1, nf.bit_length() - 1)]
    moved = {0: node_feats}
    for mask in reversed(masks):
        if mask == masks[0]:
            ahead = {0: node_feats, mask: swap(node_feats, "feat", mask)}
            ahead |= {m: piece for m, piece in moved.items() if m}
            order = sorted(ahead, reverse=True)
            moved = dict(zip(order, lax.optimization_barrier((*[ahead[m] for m in order], adj))))
            moved |= {m | mask: swap(moved[m], "feat", mask) for m in order if m and m != mask}
        else:
            moved |= {m | mask: swap(piece, "feat", mask) for m, piece in moved.items()}
    moved[0] = mine
    late = [m for m in moved if m & masks[0] and m != masks[0]]
    moved |= dict(zip(late, lax.optimization_barrier((*[moved[m] for m in late], near))))
    pieces = []
    for m in sorted(moved):
        pieces += [moved[m], swap(moved[m], "feat", 1)]
    near_2 = swap(far, "feat", 1)
    hidden, own = call(
        functools.partial(forward_kernel, nf),
        [sds((rows, width), BF), sds((rows, width), F32)],
        [VMEM] * (nf + 2),
        (*pieces, near, far),
        flops=4 * rows * depth * width,
    )
    gathered = [hidden] + [swap(hidden, "rows", j) for j in range(1, nr)]
    (feats_t,) = call(
        functools.partial(transpose_kernel, nf),
        [sds((depth, rows), BF)],
        [VMEM] * nf,
        pieces,
    )
    grad_pre, kept, *sent = call(
        functools.partial(aggregate_kernel, nr),
        [sds((rows, width), BF), sds((rows, width), F32)] + [sds((rows, width), BF)] * (nr - 1),
        [VMEM] * (nr + 4),
        (*gathered, adj, adj_t, own, grad_out),
        flops=4 * rows * nodes * width,
        limit=max(32 * 1024 * 1024, 10 * rows * nodes),
    )
    pre_2 = swap(grad_pre, "feat", 1)
    sums = [kept] + [swap(part, "rows", j + 1) for j, part in enumerate(sent)]
    (grad_hidden,) = call(
        functools.partial(sum_kernel, nr), [sds((rows, width), BF)], [VMEM] * nr, sums
    )
    hidden_2 = swap(grad_hidden, "feat", 1)
    parts = call(
        functools.partial(feats_kernel, nz),
        [sds((rows, width), BF if k else F32) for k in range(nz)],
        [VMEM] * 6,
        (grad_hidden, grad_pre, hidden_2, pre_2, near, near_2),
        flops=4 * rows * depth * width,
    )
    grads = call(
        weights_kernel,
        [sds((depth, width), BF)] * 2,
        [VMEM] * 3,
        (feats_t, grad_hidden, grad_pre),
        flops=4 * rows * depth * width,
    )
    sums_f = [parts[0]] + [swap(part, "feat", 2 * k) for k, part in enumerate(parts) if k]
    steps = [1 << bit for bit in range(nr.bit_length() - 1)]
    *between, final = zip(reversed(steps), steps)
    for there, back in between:
        other = swap(grads[0], "rows", there), swap(grads[1], "rows", back)
        grads = call(
            pair_sum_kernel,
            [sds((depth, width), BF)] * 2,
            [VMEM] * 4,
            (grads[0], other[0], grads[1], other[1]),
        )

    def finish(grads):
        other = swap(grads[0], "rows", final[0]), swap(grads[1], "rows", final[1])
        return tuple(
            call(
                pair_sum_kernel,
                [sds((depth, width), F32)] * 2,
                [VMEM] * 4,
                (grads[0], other[0], grads[1], other[1]),
            )
        )

    def skip(grads):
        return (jnp.zeros((depth, width), F32),) * 2

    grad_weight, grad_root = lax.cond(block_counts[0] > 0, finish, skip, tuple(grads))
    *sums_f, grad_weight, grad_root = lax.optimization_barrier((*sums_f, grad_weight, grad_root))
    (grad_feats,) = call(
        functools.partial(sum_kernel, len(sums_f)), [sds((rows, width), BF)], [VMEM] * len(sums_f), sums_f
    )
    return grad_feats, grad_weight, grad_root


def solution(mesh):
    placed = (
        P("rows", "feat"),
        P(None, "feat"),
        P(None, "feat"),
        P("rows", "feat"),
        P("rows"),
        P("rows"),
        P("rows", None, None),
    )
    return jax.shard_map(
        on_device,
        mesh=mesh,
        in_specs=placed,
        out_specs=(P("rows", "feat"), P(None, "feat"), P(None, "feat")),
        check_vma=False,
    )
```

```python
import functools

import jax
import jax.numpy as jnp
from jax import lax
from jax.experimental import pallas as pl
from jax.experimental.pallas import tpu as pltpu
from jax.sharding import PartitionSpec as P

BF = jnp.bfloat16
F32 = jnp.float32
VMEM = pl.BlockSpec(memory_space=pltpu.VMEM)
SMEM = pl.BlockSpec(memory_space=pltpu.SMEM)
HBM = pl.BlockSpec(memory_space=pltpu.HBM)


def dot(a, b):
    return jnp.dot(a, b, preferred_element_type=F32)


def dot_nt(a, b):
    return lax.dot_general(a, b, (((1,), (1,)), ((), ())), preferred_element_type=F32)


def call(body, outs, specs, args, flops=0, scratch=(), limit=None):
    moved = sum(a.size * a.dtype.itemsize for a in args)
    moved += sum(o.size * o.dtype.itemsize for o in outs)
    return pl.pallas_call(
        body,
        out_shape=outs,
        in_specs=specs,
        out_specs=[VMEM] * len(outs),
        scratch_shapes=scratch,
        compiler_params=pltpu.CompilerParams(vmem_limit_bytes=limit or 32 * 1024 * 1024),
        cost_estimate=pl.CostEstimate(flops=flops, bytes_accessed=moved, transcendentals=0),
    )(*args)


def sds(shape, dtype):
    return jax.ShapeDtypeStruct(shape, dtype)


def assemble_kernel(all_counts, all_cols, vals, adj, counts, cols, tiles, acc, sems):
    nblocks = counts.shape[0]
    tile = vals.shape[1]
    pairs = ((all_counts, counts), (all_cols, cols), (vals, tiles))
    copies = [pltpu.make_async_copy(*pair, sems.at[i]) for i, pair in enumerate(pairs)]
    for copy in copies:
        copy.start()
    acc[...] = jnp.zeros_like(acc)
    for copy in copies:
        copy.wait()
    start = jnp.int32(0)
    for b in range(nblocks):
        rows = slice(b * tile, (b + 1) * tile)

        def add(t, carry, rows=rows):
            place = pl.ds(pl.multiple_of(cols[t] * tile, tile), tile)
            acc[rows, place] += tiles[t].astype(F32)
            return carry

        end = start + counts[b]
        lax.fori_loop(start, end, add, 0)
        start = end
    adj[...] = acc[...].astype(BF)


def flip_kernel(tile, adj, adj_t):
    def flip(c, carry):
        place = pl.ds(pl.multiple_of(c * tile, tile), tile)
        adj_t[place, :] = adj[:, place].T
        return carry

    lax.fori_loop(0, adj.shape[1] // tile, flip, 0)


def prepare_kernel(nf, feats, weight, root, mine, near, far):
    width = weight.shape[1]
    me = lax.axis_index("feat")
    mine[...] = feats[...]
    for k in range(nf // 2):
        place = slice(k * width, (k + 1) * width)
        for flip, out in ((0, near), (1, far)):
            rows = pl.ds(pl.multiple_of((me ^ (2 * k + flip)) * width, width), width)
            out[0, place, :] = weight[rows, :]
            out[1, place, :] = root[rows, :]


def forward_kernel(nf, *refs):
    pieces, (near, far, hidden, own) = refs[:nf], refs[nf:]
    width = hidden.shape[1]
    total = None
    for k in range(nf // 2):
        place = slice(k * width, (k + 1) * width)
        left = jnp.concatenate([pieces[2 * k][...], pieces[2 * k + 1][...]], 1)
        top = jnp.concatenate([near[0, place, :], near[1, place, :]], 1)
        bottom = jnp.concatenate([far[0, place, :], far[1, place, :]], 1)
        part = dot(left, jnp.concatenate([top, bottom], 0))
        total = part if total is None else total + part
    hidden[...] = total[:, :width].astype(BF)
    own[...] = total[:, width:]


def transpose_kernel(nf, *refs):
    pieces, out = refs[:nf], refs[nf]
    me = lax.axis_index("feat")
    width = pieces[0].shape[1]
    for m in range(nf):
        rows = pl.ds(pl.multiple_of((me ^ m) * width, width), width)
        out[rows, :] = pieces[m][...].T


def begin_kernel(adj, hidden, own, pre):
    rows = own.shape[0]
    place = pl.ds(pl.multiple_of(lax.axis_index("rows") * rows, rows), rows)
    pre[...] = own[...] + dot(adj[:, place], hidden[...])


def aggregate_kernel(nr, *refs):
    hidden = refs[: nr - 1]
    adj, adj_t, begun, grad_out, grad_pre = refs[nr - 1 : nr + 4]
    sent = refs[nr + 4 :]
    me = lax.axis_index("rows")
    rows = begun.shape[0]
    pre = begun[...]
    for j in range(1, nr):
        place = pl.ds(pl.multiple_of((me ^ j) * rows, rows), rows)
        pre = pre + dot(adj[:, place], hidden[j - 1][...])
    sig = jax.nn.sigmoid(pre)
    grad = (grad_out[...].astype(F32) * sig * (1.0 + pre * (1.0 - sig))).astype(BF)
    grad_pre[...] = grad
    for j in range(1, nr):
        place = pl.ds(pl.multiple_of((me ^ j) * rows, rows), rows)
        sent[j - 1][...] = dot(adj_t[place, :], grad).astype(BF)


def keep_kernel(adj_t, grad_pre, feats_t, kept, top, bottom):
    rows = kept.shape[0]
    place = pl.ds(pl.multiple_of(lax.axis_index("rows") * rows, rows), rows)
    kept[...] = dot(adj_t[place, :], grad_pre[...])
    weights_kernel(feats_t, grad_pre, top, bottom)


def sum_kernel(n, *refs):
    total = refs[0][...].astype(F32)
    for ref in refs[1:n]:
        total = total + ref[...].astype(F32)
    refs[n][...] = total.astype(refs[n].dtype)


def feats_kernel(nz, hidden, pre, hidden_2, pre_2, near, near_2, *out):
    width = hidden.shape[1]
    left = jnp.concatenate([hidden[...], pre[...], hidden_2[...], pre_2[...]], 1)
    for k in range(nz):
        place = slice(k * width, (k + 1) * width)
        right = [near[0, place, :], near[1, place, :], near_2[0, place, :], near_2[1, place, :]]
        out[k][...] = dot_nt(left, jnp.concatenate(right, 1)).astype(out[k].dtype)


def weights_kernel(feats_t, grads, top, bottom):
    half = top.shape[0]
    top[...] = dot(feats_t[:half, :], grads[...]).astype(BF)
    bottom[...] = dot(feats_t[half:, :], grads[...]).astype(BF)


def join_kernel(*refs):
    terms, outs = refs[:8], refs[8:]
    for half, out in enumerate(outs):
        weight = terms[half][...].astype(F32) + terms[half + 2][...].astype(F32)
        root = terms[half + 4][...].astype(F32) + terms[half + 6][...].astype(F32)
        out[...] = jnp.concatenate([weight, root], 1).astype(BF)


def pair_sum_kernel(top, top_2, bottom, bottom_2, top_sum, bottom_sum):
    for out, terms in ((top_sum, (top, top_2)), (bottom_sum, (bottom, bottom_2))):
        total = terms[0][...].astype(F32) + terms[1][...].astype(F32)
        out[...] = total.astype(BF)


def place_kernel(top, top_2, bottom, bottom_2, weight, root):
    half, width = top.shape[0], weight.shape[1]
    for at, terms in ((0, (top, top_2)), (half, (bottom, bottom_2))):
        total = terms[0][...].astype(F32) + terms[1][...].astype(F32)
        weight[at : at + half, :] = total[:, :width]
        root[at : at + half, :] = total[:, width:]


def on_device(node_feats, weight, root_weight, grad_out, block_counts, tile_cols, tile_vals):
    rows, width = node_feats.shape
    depth = weight.shape[0]
    nr, nf = lax.axis_size("rows"), lax.axis_size("feat")
    nz = nf // 2
    nodes = rows * nr

    def swap(array, axis, mask):
        return lax.ppermute(array, axis, [(i, i ^ mask) for i in range(lax.axis_size(axis))])

    (adj,) = call(
        assemble_kernel,
        [sds((rows, nodes), BF)],
        [HBM] * 3,
        (block_counts, tile_cols, tile_vals),
        flops=4 * rows * nodes,
        scratch=[
            pltpu.SMEM(block_counts.shape, jnp.int32),
            pltpu.SMEM(tile_cols.shape, jnp.int32),
            pltpu.VMEM(tile_vals.shape, BF),
            pltpu.VMEM((rows, nodes), F32),
            pltpu.SemaphoreType.DMA((3,)),
        ],
        limit=58 * 1024 * 1024,
    )
    mine, near, far = call(
        functools.partial(prepare_kernel, nf),
        [sds((rows, width), BF)] + [sds((2, depth // 2, width), BF)] * 2,
        [VMEM] * 3,
        (node_feats, weight, root_weight),
    )
    (adj_t,) = call(
        functools.partial(flip_kernel, tile_vals.shape[1]), [sds((nodes, rows), BF)], [VMEM], (adj,)
    )
    ranks = sorted(range(1, nz), key=lambda k: (k < nz // 2, k))
    moved = {0: node_feats} | {2 * k: swap(node_feats, "feat", 2 * k) for k in ranks}
    order = [2 * k for k in ranks]
    moved |= dict(zip(order, lax.optimization_barrier((*[moved[m] for m in order], adj))))
    moved[0] = mine
    late = [m for m in moved if m == 2 * nz - 2]
    moved |= dict(zip(late, lax.optimization_barrier((*[moved[m] for m in late], near))))
    pieces = []
    for m in sorted(moved):
        pieces += [moved[m], swap(moved[m], "feat", 1)]
    near_2 = swap(far, "feat", 1)
    hidden, own = call(
        functools.partial(forward_kernel, nf),
        [sds((rows, width), BF), sds((rows, width), F32)],
        [VMEM] * (nf + 2),
        (*pieces, near, far),
        flops=4 * rows * depth * width,
    )
    gathered = [hidden] + [swap(hidden, "rows", j) for j in range(1, nr)]
    (feats_t,) = call(
        functools.partial(transpose_kernel, nf),
        [sds((depth, rows), BF)],
        [VMEM] * nf,
        pieces,
    )
    adj_t, near_2 = lax.optimization_barrier((adj_t, near_2))
    (begun,) = call(
        begin_kernel,
        [sds((rows, width), F32)],
        [VMEM] * 3,
        (adj, hidden, own),
        flops=2 * rows * rows * width,
    )
    grad_pre, *sent = call(
        functools.partial(aggregate_kernel, nr),
        [sds((rows, width), BF)] * nr,
        [VMEM] * (nr + 3),
        (*gathered[1:], adj, adj_t, begun, grad_out),
        flops=4 * rows * nodes * width,
        limit=max(32 * 1024 * 1024, 10 * rows * nodes),
    )
    kept, *root_part = call(
        keep_kernel,
        [sds((rows, width), F32)] + [sds((depth // 2, width), BF)] * 2,
        [VMEM] * 3,
        (adj_t, grad_pre, feats_t),
        flops=4 * rows * depth * width,
    )
    pre_2 = swap(grad_pre, "feat", 1)
    sums = [kept] + [swap(part, "rows", j + 1) for j, part in enumerate(sent)]
    (grad_hidden,) = call(
        functools.partial(sum_kernel, nr), [sds((rows, width), BF)], [VMEM] * nr, sums
    )
    hidden_2 = swap(grad_hidden, "feat", 1)
    parts = call(
        functools.partial(feats_kernel, nz),
        [sds((rows, width), BF if k else F32) for k in range(nz)],
        [VMEM] * 6,
        (grad_hidden, grad_pre, hidden_2, pre_2, near, near_2),
        flops=4 * rows * depth * width,
    )
    weight_part = call(
        weights_kernel,
        [sds((depth // 2, width), BF)] * 2,
        [VMEM] * 2,
        (feats_t, grad_hidden),
        flops=2 * rows * depth * width,
    )
    steps = [1 << bit for bit in range(nr.bit_length() - 1)]
    first, *between, final = zip(steps, reversed(steps))
    root_got = [swap(part, "rows", mask) for part, mask in zip(root_part, first)]
    *weight_part, root_got[0], root_got[1] = lax.optimization_barrier((*weight_part, *root_got))
    weight_got = [swap(part, "rows", mask) for part, mask in zip(weight_part, first)]
    sums_f = [parts[0]] + [swap(parts[k], "feat", 2 * k) for k in ranks]
    joined = [sds((depth // 2, 2 * width), BF)] * 2
    grads = call(
        join_kernel, joined, [VMEM] * 8, (*weight_part, *weight_got, *root_part, *root_got)
    )
    for masks in between:
        got = [swap(part, "rows", mask) for part, mask in zip(grads, masks)]
        grads = call(pair_sum_kernel, joined, [VMEM] * 4, (grads[0], got[0], grads[1], got[1]))

    def finish(grads):
        got = [swap(part, "rows", mask) for part, mask in zip(grads, final)]
        return tuple(
            call(
                place_kernel,
                [sds((depth, width), F32)] * 2,
                [VMEM] * 4,
                (grads[0], got[0], grads[1], got[1]),
            )
        )

    def skip(grads):
        return (jnp.zeros((depth, width), F32),) * 2

    grad_weight, grad_root = lax.cond(block_counts[0] > 0, finish, skip, tuple(grads))
    *sums_f, grad_weight, grad_root = lax.optimization_barrier((*sums_f, grad_weight, grad_root))
    (grad_feats,) = call(
        functools.partial(sum_kernel, len(sums_f)),
        [sds((rows, width), BF)],
        [VMEM] * len(sums_f),
        sums_f,
    )
    return grad_feats, grad_weight, grad_root


def solution(mesh):
    placed = (
        P("rows", "feat"),
        P(None, "feat"),
        P(None, "feat"),
        P("rows", "feat"),
        P("rows"),
        P("rows"),
        P("rows", None, None),
    )
    return jax.shard_map(
        on_device,
        mesh=mesh,
        in_specs=placed,
        out_specs=(P("rows", "feat"), P(None, "feat"), P(None, "feat")),
        check_vma=False,
    )
```

```python
import functools

import jax
import jax.numpy as jnp
from jax import lax
from jax.experimental import pallas as pl
from jax.experimental.pallas import tpu as pltpu
from jax.sharding import PartitionSpec as P

BF = jnp.bfloat16
F32 = jnp.float32
VMEM = pl.BlockSpec(memory_space=pltpu.VMEM)
SMEM = pl.BlockSpec(memory_space=pltpu.SMEM)
HBM = pl.BlockSpec(memory_space=pltpu.HBM)


def dot(a, b):
    return jnp.dot(a, b, preferred_element_type=F32)


def dot_nt(a, b):
    return lax.dot_general(a, b, (((1,), (1,)), ((), ())), preferred_element_type=F32)


def call(body, outs, specs, args, flops=0, scratch=(), limit=None):
    moved = sum(a.size * a.dtype.itemsize for a in args)
    moved += sum(o.size * o.dtype.itemsize for o in outs)
    return pl.pallas_call(
        body,
        out_shape=outs,
        in_specs=specs,
        out_specs=[VMEM] * len(outs),
        scratch_shapes=scratch,
        compiler_params=pltpu.CompilerParams(vmem_limit_bytes=limit or 32 * 1024 * 1024),
        cost_estimate=pl.CostEstimate(flops=flops, bytes_accessed=moved, transcendentals=0),
    )(*args)


def sds(shape, dtype):
    return jax.ShapeDtypeStruct(shape, dtype)


def assemble_kernel(all_counts, all_cols, vals, adj, counts, cols, tiles, acc, sems):
    nblocks = counts.shape[0]
    tile = vals.shape[1]
    pairs = ((all_counts, counts), (all_cols, cols), (vals, tiles))
    copies = [pltpu.make_async_copy(*pair, sems.at[i]) for i, pair in enumerate(pairs)]
    for copy in copies:
        copy.start()
    acc[...] = jnp.zeros_like(acc)
    for copy in copies:
        copy.wait()
    start = jnp.int32(0)
    for b in range(nblocks):
        rows = slice(b * tile, (b + 1) * tile)

        def add(t, carry, rows=rows):
            place = pl.ds(pl.multiple_of(cols[t] * tile, tile), tile)
            acc[rows, place] += tiles[t].astype(F32)
            return carry

        end = start + counts[b]
        lax.fori_loop(start, end, add, 0)
        start = end
    adj[...] = acc[...].astype(BF)


def flip_kernel(tile, adj, adj_t):
    def flip(c, carry):
        place = pl.ds(pl.multiple_of(c * tile, tile), tile)
        adj_t[place, :] = adj[:, place].T
        return carry

    lax.fori_loop(0, adj.shape[1] // tile, flip, 0)


def prepare_kernel(nf, feats, weight, root, mine, near, far):
    width = weight.shape[1]
    me = lax.axis_index("feat")
    mine[...] = feats[...]
    for k in range(nf // 2):
        place = slice(k * width, (k + 1) * width)
        for flip, out in ((0, near), (1, far)):
            rows = pl.ds(pl.multiple_of((me ^ (2 * k + flip)) * width, width), width)
            out[0, place, :] = weight[rows, :]
            out[1, place, :] = root[rows, :]


def forward_kernel(nf, *refs):
    pieces, (near, far, hidden, own) = refs[:nf], refs[nf:]
    width = hidden.shape[1]
    total = None
    for k in range(nf // 2):
        place = slice(k * width, (k + 1) * width)
        left = jnp.concatenate([pieces[2 * k][...], pieces[2 * k + 1][...]], 1)
        top = jnp.concatenate([near[0, place, :], near[1, place, :]], 1)
        bottom = jnp.concatenate([far[0, place, :], far[1, place, :]], 1)
        part = dot(left, jnp.concatenate([top, bottom], 0))
        total = part if total is None else total + part
    hidden[...] = total[:, :width].astype(BF)
    own[...] = total[:, width:]


def transpose_kernel(nf, *refs):
    pieces, out = refs[:nf], refs[nf]
    me = lax.axis_index("feat")
    width = pieces[0].shape[1]
    for m in range(nf):
        rows = pl.ds(pl.multiple_of((me ^ m) * width, width), width)
        out[rows, :] = pieces[m][...].T


def begin_kernel(adj, hidden, own, pre):
    rows = own.shape[0]
    place = pl.ds(pl.multiple_of(lax.axis_index("rows") * rows, rows), rows)
    pre[...] = own[...] + dot(adj[:, place], hidden[...])


def aggregate_kernel(nr, *refs):
    hidden = refs[: nr - 1]
    adj, adj_t, begun, grad_out, grad_pre = refs[nr - 1 : nr + 4]
    sent = refs[nr + 4 :]
    me = lax.axis_index("rows")
    rows = begun.shape[0]
    pre = begun[...]
    for j in range(1, nr):
        place = pl.ds(pl.multiple_of((me ^ j) * rows, rows), rows)
        pre = pre + dot(adj[:, place], hidden[j - 1][...])
    sig = jax.nn.sigmoid(pre)
    grad = (grad_out[...].astype(F32) * sig * (1.0 + pre * (1.0 - sig))).astype(BF)
    grad_pre[...] = grad
    for j in range(1, nr):
        place = pl.ds(pl.multiple_of((me ^ j) * rows, rows), rows)
        sent[j - 1][...] = dot(adj_t[place, :], grad).astype(BF)


def keep_kernel(adj_t, grad_pre, feats_t, kept, top, bottom):
    rows = kept.shape[0]
    place = pl.ds(pl.multiple_of(lax.axis_index("rows") * rows, rows), rows)
    kept[...] = dot(adj_t[place, :], grad_pre[...])
    weights_kernel(feats_t, grad_pre, top, bottom)


def sum_kernel(n, *refs):
    total = refs[0][...].astype(F32)
    for ref in refs[1:n]:
        total = total + ref[...].astype(F32)
    refs[n][...] = total.astype(refs[n].dtype)


def feats_kernel(nz, hidden, pre, hidden_2, pre_2, near, near_2, *out):
    width = hidden.shape[1]
    left = jnp.concatenate([hidden[...], pre[...], hidden_2[...], pre_2[...]], 1)
    for k in range(nz):
        place = slice(k * width, (k + 1) * width)
        right = [near[0, place, :], near[1, place, :], near_2[0, place, :], near_2[1, place, :]]
        out[k][...] = dot_nt(left, jnp.concatenate(right, 1)).astype(out[k].dtype)


def weights_kernel(feats_t, grads, top, bottom):
    half = top.shape[0]
    top[...] = dot(feats_t[:half, :], grads[...]).astype(BF)
    bottom[...] = dot(feats_t[half:, :], grads[...]).astype(BF)


def join_kernel(*refs):
    terms, outs = refs[:6], refs[6:]
    for half, out in enumerate(outs):
        width = out.shape[1] // 2
        out[:, :width] = terms[half][...]
        root = terms[half + 2][...].astype(F32) + terms[half + 4][...].astype(F32)
        out[:, width:] = root.astype(BF)


def pair_sum_kernel(top, top_2, bottom, bottom_2, top_sum, bottom_sum):
    for out, terms in ((top_sum, (top, top_2)), (bottom_sum, (bottom, bottom_2))):
        width = out.shape[1]
        total = terms[0][:, :width].astype(F32) + terms[1][:, :width].astype(F32)
        out[...] = total.astype(BF)


def place_kernel(top, top_2, bottom, bottom_2, out):
    half, width = top.shape[0], out.shape[1]
    for at, terms in ((0, (top, top_2)), (half, (bottom, bottom_2))):
        total = terms[0][...].astype(F32) + terms[1][...].astype(F32)
        out[at : at + half, :] = total[:, -width:]


def on_device(node_feats, weight, root_weight, grad_out, block_counts, tile_cols, tile_vals):
    rows, width = node_feats.shape
    depth = weight.shape[0]
    nr, nf = lax.axis_size("rows"), lax.axis_size("feat")
    nz = nf // 2
    nodes = rows * nr

    def swap(array, axis, mask):
        return lax.ppermute(array, axis, [(i, i ^ mask) for i in range(lax.axis_size(axis))])

    (adj,) = call(
        assemble_kernel,
        [sds((rows, nodes), BF)],
        [HBM] * 3,
        (block_counts, tile_cols, tile_vals),
        flops=4 * rows * nodes,
        scratch=[
            pltpu.SMEM(block_counts.shape, jnp.int32),
            pltpu.SMEM(tile_cols.shape, jnp.int32),
            pltpu.VMEM(tile_vals.shape, BF),
            pltpu.VMEM((rows, nodes), F32),
            pltpu.SemaphoreType.DMA((3,)),
        ],
        limit=48 * 1024 * 1024,
    )
    mine, near, far = call(
        functools.partial(prepare_kernel, nf),
        [sds((rows, width), BF)] + [sds((2, depth // 2, width), BF)] * 2,
        [VMEM] * 3,
        (node_feats, weight, root_weight),
    )
    (adj_t,) = call(
        functools.partial(flip_kernel, tile_vals.shape[1]), [sds((nodes, rows), BF)], [VMEM], (adj,)
    )
    ranks = sorted(range(1, nz), key=lambda k: (k < nz // 2, k))
    masks = [1 << bit for bit in range(1, nf.bit_length() - 1)]
    moved = {0: node_feats}
    for mask in reversed(masks[1:]):
        moved |= {m | mask: swap(piece, "feat", mask) for m, piece in moved.items()}
    moved[masks[0]] = swap(node_feats, "feat", masks[0])
    beside = {0: swap(node_feats, "feat", 1)}
    order = sorted((m for m in moved if m), reverse=True)
    *early, near, beside[0] = lax.optimization_barrier((*[moved[m] for m in order], near, beside[0]))
    moved |= dict(zip(order, early))
    ahead = {m: swap(moved[m], "feat", 1) for m in order}
    last = [m | masks[0] for m in order if m != masks[0]]
    moved |= {m: swap(moved[m ^ masks[0]], "feat", masks[0]) for m in last}
    held = lax.optimization_barrier((*[moved[m] for m in last], *[ahead[m] for m in order]))
    moved |= dict(zip(last, held))
    beside |= dict(zip(order, held[len(last) :]))
    beside |= {m: swap(moved[m], "feat", 1) for m in last}
    moved[0] = mine
    pieces = [piece for m in sorted(moved) for piece in (moved[m], beside[m])]
    near_2 = swap(far, "feat", 1)
    hidden, own = call(
        functools.partial(forward_kernel, nf),
        [sds((rows, width), BF), sds((rows, width), F32)],
        [VMEM] * (nf + 2),
        (*pieces, near, far),
        flops=4 * rows * depth * width,
    )
    gathered = [hidden] + [swap(hidden, "rows", j) for j in range(1, nr)]
    (feats_t,) = call(
        functools.partial(transpose_kernel, nf),
        [sds((depth, rows), BF)],
        [VMEM] * nf,
        pieces,
    )
    adj_t, near_2 = lax.optimization_barrier((adj_t, near_2))
    (begun,) = call(
        begin_kernel,
        [sds((rows, width), F32)],
        [VMEM] * 3,
        (adj, hidden, own),
        flops=2 * rows * rows * width,
    )
    grad_pre, *sent = call(
        functools.partial(aggregate_kernel, nr),
        [sds((rows, width), BF)] * nr,
        [VMEM] * (nr + 3),
        (*gathered[1:], adj, adj_t, begun, grad_out),
        flops=4 * rows * nodes * width,
        limit=max(32 * 1024 * 1024, 10 * rows * nodes),
    )
    kept, *root_part = call(
        keep_kernel,
        [sds((rows, width), F32)] + [sds((depth // 2, width), BF)] * 2,
        [VMEM] * 3,
        (adj_t, grad_pre, feats_t),
        flops=4 * rows * depth * width,
    )
    pre_2 = swap(grad_pre, "feat", 1)
    sums = [kept] + [swap(part, "rows", j + 1) for j, part in enumerate(sent)]
    (grad_hidden,) = call(
        functools.partial(sum_kernel, nr), [sds((rows, width), BF)], [VMEM] * nr, sums
    )
    hidden_2 = swap(grad_hidden, "feat", 1)
    parts = call(
        functools.partial(feats_kernel, nz),
        [sds((rows, width), BF if k else F32) for k in range(nz)],
        [VMEM] * 6,
        (grad_hidden, grad_pre, hidden_2, pre_2, near, near_2),
        flops=4 * rows * depth * width,
    )
    weight_part = call(
        weights_kernel,
        [sds((depth // 2, width), BF)] * 2,
        [VMEM] * 2,
        (feats_t, grad_hidden),
        flops=2 * rows * depth * width,
    )
    steps = [1 << bit for bit in range(nr.bit_length() - 1)]
    first, *between = zip(steps, reversed(steps))
    final = between[-1]
    root_got = [swap(part, "rows", mask) for part, mask in zip(root_part, first)]
    *weight_part, root_got[0], root_got[1] = lax.optimization_barrier((*weight_part, *root_got))
    sums_f = [parts[0]] + [swap(parts[k], "feat", 2 * k) for k in ranks]
    joined = [sds((depth // 2, 2 * width), BF)] * 2
    grads = call(join_kernel, joined, [VMEM] * 6, (*weight_part, *root_part, *root_got))
    for masks in between:
        got = [swap(part, "rows", mask) for part, mask in zip(grads, masks)]
        pairs = grads[0], got[0], grads[1], got[1]
        last = masks == final
        shapes = [sds((depth // 2, width), BF)] * 2 if last else joined
        grads = call(pair_sum_kernel, shapes, [VMEM] * 4, pairs)

    def place(top, top_2, bottom, bottom_2):
        arrays = top, top_2, bottom, bottom_2
        return call(place_kernel, [sds((depth, width), F32)], [VMEM] * 4, arrays)[0]

    def finish(operands):
        grads, pairs = operands
        got = [swap(part, "rows", mask) for part, mask in zip(grads, first)]
        return place(grads[0], got[0], grads[1], got[1]), place(*pairs)

    def skip(operands):
        return (jnp.zeros((depth, width), F32),) * 2

    operands = tuple(grads), tuple(pairs)
    grad_weight, grad_root = lax.cond(block_counts[0] > 0, finish, skip, operands)
    *sums_f, grad_weight, grad_root = lax.optimization_barrier((*sums_f, grad_weight, grad_root))
    (grad_feats,) = call(
        functools.partial(sum_kernel, len(sums_f)),
        [sds((rows, width), BF)],
        [VMEM] * len(sums_f),
        sums_f,
    )
    return grad_feats, grad_weight, grad_root


def solution(mesh):
    placed = (
        P("rows", "feat"),
        P(None, "feat"),
        P(None, "feat"),
        P("rows", "feat"),
        P("rows"),
        P("rows"),
        P("rows", None, None),
    )
    return jax.shard_map(
        on_device,
        mesh=mesh,
        in_specs=placed,
        out_specs=(P("rows", "feat"), P(None, "feat"), P(None, "feat")),
        check_vma=False,
    )
```

```python
import functools

import jax
import jax.numpy as jnp
from jax import lax
from jax.experimental import pallas as pl
from jax.experimental.pallas import tpu as pltpu
from jax.sharding import PartitionSpec as P

BF = jnp.bfloat16
F32 = jnp.float32
VMEM = pl.BlockSpec(memory_space=pltpu.VMEM)
SMEM = pl.BlockSpec(memory_space=pltpu.SMEM)
HBM = pl.BlockSpec(memory_space=pltpu.HBM)


def dot(a, b):
    return jnp.dot(a, b, preferred_element_type=F32)


def dot_nt(a, b):
    return lax.dot_general(a, b, (((1,), (1,)), ((), ())), preferred_element_type=F32)


def call(body, outs, specs, args, flops=0, scratch=(), limit=None):
    moved = sum(a.size * a.dtype.itemsize for a in args)
    moved += sum(o.size * o.dtype.itemsize for o in outs)
    return pl.pallas_call(
        body,
        out_shape=outs,
        in_specs=specs,
        out_specs=[VMEM] * len(outs),
        scratch_shapes=scratch,
        compiler_params=pltpu.CompilerParams(vmem_limit_bytes=limit or 32 * 1024 * 1024),
        cost_estimate=pl.CostEstimate(flops=flops, bytes_accessed=moved, transcendentals=0),
    )(*args)


def sds(shape, dtype):
    return jax.ShapeDtypeStruct(shape, dtype)


def assemble_kernel(all_counts, all_cols, vals, adj, counts, cols, tiles, acc, sems):
    nblocks = counts.shape[0]
    tile = vals.shape[1]
    pairs = ((all_counts, counts), (all_cols, cols), (vals, tiles))
    copies = [pltpu.make_async_copy(*pair, sems.at[i]) for i, pair in enumerate(pairs)]
    for copy in copies:
        copy.start()
    acc[...] = jnp.zeros_like(acc)
    for copy in copies:
        copy.wait()
    start = jnp.int32(0)
    for b in range(nblocks):
        rows = slice(b * tile, (b + 1) * tile)

        def add(t, carry, rows=rows):
            place = pl.ds(pl.multiple_of(cols[t] * tile, tile), tile)
            acc[rows, place] += tiles[t].astype(F32)
            return carry

        end = start + counts[b]
        lax.fori_loop(start, end, add, 0)
        start = end
    adj[...] = acc[...].astype(BF)


def flip_kernel(tile, adj, adj_t):
    def flip(c, carry):
        place = pl.ds(pl.multiple_of(c * tile, tile), tile)
        adj_t[place, :] = adj[:, place].T
        return carry

    lax.fori_loop(0, adj.shape[1] // tile, flip, 0)


def prepare_kernel(nf, feats, weight, root, mine, near, far, right):
    width = weight.shape[1]
    me = lax.axis_index("feat")
    mine[...] = feats[...]
    for k in range(nf // 2):
        place = slice(k * width, (k + 1) * width)
        for flip, out in ((0, near), (1, far)):
            rows = pl.ds(pl.multiple_of((me ^ (2 * k + flip)) * width, width), width)
            out[0, place, :] = weight[rows, :]
            out[1, place, :] = root[rows, :]
            into = slice((2 * k + flip) * width, (2 * k + flip + 1) * width)
            right[into, :] = jnp.concatenate([weight[rows, :], root[rows, :]], 1)


def forward_kernel(nf, *refs):
    pieces, (right, hidden, own) = refs[:nf], refs[nf:]
    rows, width = hidden.shape
    half = rows // 2
    for at in (0, half):
        part = slice(at, at + half)
        left = jnp.concatenate([piece[part, :] for piece in pieces], 1)
        total = dot(left, right[...])
        hidden[part, :] = total[:, :width].astype(BF)
        own[part, :] = total[:, width:]


def transpose_kernel(nf, *refs):
    pieces, out = refs[:nf], refs[nf]
    me = lax.axis_index("feat")
    width = pieces[0].shape[1]
    for m in range(nf):
        rows = pl.ds(pl.multiple_of((me ^ m) * width, width), width)
        out[rows, :] = pieces[m][...].T


def begin_kernel(adj, hidden, own, pre):
    rows = own.shape[0]
    place = pl.ds(pl.multiple_of(lax.axis_index("rows") * rows, rows), rows)
    pre[...] = own[...] + dot(adj[:, place], hidden[...])


def aggregate_kernel(nr, *refs):
    hidden = refs[: nr - 1]
    adj, adj_t, begun, grad_out, grad_pre = refs[nr - 1 : nr + 4]
    sent = refs[nr + 4 :]
    me = lax.axis_index("rows")
    rows = begun.shape[0]
    places = [pl.ds(pl.multiple_of((me ^ j) * rows, rows), rows) for j in range(1, nr)]
    half = rows // 2
    for at in (0, half):
        part = slice(at, at + half)
        pre = begun[part, :]
        for j in range(nr - 1):
            pre = pre + dot(adj[part, places[j]], hidden[j][...])
        sig = jax.nn.sigmoid(pre)
        grad = grad_out[part, :].astype(F32) * sig * (1.0 + pre * (1.0 - sig))
        grad_pre[part, :] = grad.astype(BF)
    for j in range(nr - 1):
        sent[j][...] = dot(adj_t[places[j], :], grad_pre[...]).astype(BF)


def keep_kernel(adj_t, grad_pre, kept):
    rows = kept.shape[0]
    place = pl.ds(pl.multiple_of(lax.axis_index("rows") * rows, rows), rows)
    kept[...] = dot(adj_t[place, :], grad_pre[...])


def sum_kernel(n, *refs):
    total = refs[0][...].astype(F32)
    for ref in refs[1:n]:
        total = total + ref[...].astype(F32)
    refs[n][...] = total.astype(refs[n].dtype)


def back_kernel(nz, near, near_2, back):
    width = near.shape[2]
    for k in range(nz):
        place = slice(k * width, (k + 1) * width)
        rows = [near[0, place, :], near[1, place, :], near_2[0, place, :], near_2[1, place, :]]
        back[:, place] = jnp.concatenate(rows, 1).T


def feats_kernel(nz, hidden, pre, hidden_2, pre_2, back, *out):
    rows, width = hidden.shape
    half = rows // 2
    for at in (0, half):
        part = slice(at, at + half)
        arrays = hidden, pre, hidden_2, pre_2
        total = dot(jnp.concatenate([array[part, :] for array in arrays], 1), back[...])
        for k in range(nz):
            out[k][part, :] = total[:, k * width : (k + 1) * width].astype(out[k].dtype)


def weights_kernel(feats_t, grads, top, bottom):
    half = top.shape[0]
    step = half // 2
    for at in range(0, 2 * half, step):
        out = top if at < half else bottom
        place = slice(at % half, at % half + step)
        out[place, :] = dot(feats_t[at : at + step, :], grads[...]).astype(BF)


def join_kernel(*refs):
    terms, outs = refs[:6], refs[6:]
    for half, out in enumerate(outs):
        width = out.shape[1] // 2
        out[:, :width] = terms[half][...]
        root = terms[half + 2][...].astype(F32) + terms[half + 4][...].astype(F32)
        out[:, width:] = root.astype(BF)


def pair_sum_kernel(top, top_2, bottom, bottom_2, top_sum, bottom_sum):
    for out, terms in ((top_sum, (top, top_2)), (bottom_sum, (bottom, bottom_2))):
        width = out.shape[1]
        total = terms[0][:, :width].astype(F32) + terms[1][:, :width].astype(F32)
        out[...] = total.astype(BF)


def place_kernel(top, top_2, bottom, bottom_2, out):
    half, width = top.shape[0], out.shape[1]
    for at, terms in ((0, (top, top_2)), (half, (bottom, bottom_2))):
        total = terms[0][...].astype(F32) + terms[1][...].astype(F32)
        out[at : at + half, :] = total[:, -width:]


def on_device(node_feats, weight, root_weight, grad_out, block_counts, tile_cols, tile_vals):
    rows, width = node_feats.shape
    depth = weight.shape[0]
    nr, nf = lax.axis_size("rows"), lax.axis_size("feat")
    nz = nf // 2
    nodes = rows * nr

    def swap(array, axis, mask):
        return lax.ppermute(array, axis, [(i, i ^ mask) for i in range(lax.axis_size(axis))])

    (adj,) = call(
        assemble_kernel,
        [sds((rows, nodes), BF)],
        [HBM] * 3,
        (block_counts, tile_cols, tile_vals),
        flops=4 * rows * nodes,
        scratch=[
            pltpu.SMEM(block_counts.shape, jnp.int32),
            pltpu.SMEM(tile_cols.shape, jnp.int32),
            pltpu.VMEM(tile_vals.shape, BF),
            pltpu.VMEM((rows, nodes), F32),
            pltpu.SemaphoreType.DMA((3,)),
        ],
        limit=48 * 1024 * 1024,
    )
    mine, near, far, right = call(
        functools.partial(prepare_kernel, nf),
        [sds((rows, width), BF)]
        + [sds((2, depth // 2, width), BF)] * 2
        + [sds((depth, 2 * width), BF)],
        [VMEM] * 3,
        (node_feats, weight, root_weight),
    )
    (adj_t,) = call(
        functools.partial(flip_kernel, tile_vals.shape[1]), [sds((nodes, rows), BF)], [VMEM], (adj,)
    )
    ranks = sorted(range(1, nz), key=lambda k: (k < nz // 2, k))
    masks = [1 << bit for bit in range(1, nf.bit_length() - 1)]
    moved = {0: node_feats}
    for mask in reversed(masks[1:]):
        moved |= {m | mask: swap(piece, "feat", mask) for m, piece in moved.items()}
    moved[masks[0]] = swap(node_feats, "feat", masks[0])
    beside = {0: swap(node_feats, "feat", 1)}
    order = sorted((m for m in moved if m), reverse=True)
    *early, near, beside[0] = lax.optimization_barrier((*[moved[m] for m in order], near, beside[0]))
    moved |= dict(zip(order, early))
    ahead = {m: swap(moved[m], "feat", 1) for m in order}
    last = [m | masks[0] for m in order if m != masks[0]]
    moved |= {m: swap(moved[m ^ masks[0]], "feat", masks[0]) for m in last}
    held = lax.optimization_barrier((*[moved[m] for m in last], *[ahead[m] for m in order]))
    moved |= dict(zip(last, held))
    beside |= dict(zip(order, held[len(last) :]))
    beside |= {m: swap(moved[m], "feat", 1) for m in last}
    moved[0] = mine
    pieces = [piece for m in sorted(moved) for piece in (moved[m], beside[m])]
    near_2 = swap(far, "feat", 1)
    hidden, own = call(
        functools.partial(forward_kernel, nf),
        [sds((rows, width), BF), sds((rows, width), F32)],
        [VMEM] * (nf + 1),
        (*pieces, right),
        flops=4 * rows * depth * width,
    )
    gathered = [hidden] + [swap(hidden, "rows", j) for j in range(1, nr)]
    (feats_t,) = call(
        functools.partial(transpose_kernel, nf),
        [sds((depth, rows), BF)],
        [VMEM] * nf,
        pieces,
    )
    (back,) = call(
        functools.partial(back_kernel, nz),
        [sds((4 * width, depth // 2), BF)],
        [VMEM] * 2,
        (near, near_2),
    )
    adj_t, back, feats_t = lax.optimization_barrier((adj_t, back, feats_t))
    (begun,) = call(
        begin_kernel,
        [sds((rows, width), F32)],
        [VMEM] * 3,
        (adj, hidden, own),
        flops=2 * rows * rows * width,
    )
    grad_pre, *sent = call(
        functools.partial(aggregate_kernel, nr),
        [sds((rows, width), BF)] * nr,
        [VMEM] * (nr + 3),
        (*gathered[1:], adj, adj_t, begun, grad_out),
        flops=4 * rows * nodes * width,
        limit=max(32 * 1024 * 1024, 10 * rows * nodes),
    )
    root_part = call(
        weights_kernel,
        [sds((depth // 2, width), BF)] * 2,
        [VMEM] * 2,
        (feats_t, grad_pre),
        flops=2 * rows * depth * width,
    )
    (kept,) = call(
        keep_kernel,
        [sds((rows, width), F32)],
        [VMEM] * 2,
        (adj_t, grad_pre),
        flops=2 * rows * rows * width,
    )
    pre_2 = swap(grad_pre, "feat", 1)
    sums = [kept] + [swap(part, "rows", j + 1) for j, part in enumerate(sent)]
    (grad_hidden,) = call(
        functools.partial(sum_kernel, nr), [sds((rows, width), BF)], [VMEM] * nr, sums
    )
    hidden_2 = swap(grad_hidden, "feat", 1)
    parts = call(
        functools.partial(feats_kernel, nz),
        [sds((rows, width), BF if k else F32) for k in range(nz)],
        [VMEM] * 5,
        (grad_hidden, grad_pre, hidden_2, pre_2, back),
        flops=4 * rows * depth * width,
    )
    weight_part = call(
        weights_kernel,
        [sds((depth // 2, width), BF)] * 2,
        [VMEM] * 2,
        (feats_t, grad_hidden),
        flops=2 * rows * depth * width,
    )
    steps = [1 << bit for bit in range(nr.bit_length() - 1)]
    first, *between = zip(steps, reversed(steps))
    final = between[-1]
    root_got = [swap(part, "rows", mask) for part, mask in zip(root_part, first)]
    *weight_part, root_got[0], root_got[1] = lax.optimization_barrier((*weight_part, *root_got))
    sums_f = [parts[0]] + [swap(parts[k], "feat", 2 * k) for k in ranks]
    joined = [sds((depth // 2, 2 * width), BF)] * 2
    grads = call(join_kernel, joined, [VMEM] * 6, (*weight_part, *root_part, *root_got))
    for masks in between:
        got = [swap(part, "rows", mask) for part, mask in zip(grads, masks)]
        pairs = grads[0], got[0], grads[1], got[1]
        last = masks == final
        shapes = [sds((depth // 2, width), BF)] * 2 if last else joined
        grads = call(pair_sum_kernel, shapes, [VMEM] * 4, pairs)

    def place(top, top_2, bottom, bottom_2):
        arrays = top, top_2, bottom, bottom_2
        return call(place_kernel, [sds((depth, width), F32)], [VMEM] * 4, arrays)[0]

    def finish(operands):
        grads, pairs = operands
        got = [swap(part, "rows", mask) for part, mask in zip(grads, first)]
        return place(grads[0], got[0], grads[1], got[1]), place(*pairs)

    def skip(operands):
        return (jnp.zeros((depth, width), F32),) * 2

    operands = tuple(grads), tuple(pairs)
    grad_weight, grad_root = lax.cond(block_counts[0] > 0, finish, skip, operands)
    *sums_f, grad_weight, grad_root = lax.optimization_barrier((*sums_f, grad_weight, grad_root))
    (grad_feats,) = call(
        functools.partial(sum_kernel, len(sums_f)),
        [sds((rows, width), BF)],
        [VMEM] * len(sums_f),
        sums_f,
    )
    return grad_feats, grad_weight, grad_root


def solution(mesh):
    placed = (
        P("rows", "feat"),
        P(None, "feat"),
        P(None, "feat"),
        P("rows", "feat"),
        P("rows"),
        P("rows"),
        P("rows", None, None),
    )
    return jax.shard_map(
        on_device,
        mesh=mesh,
        in_specs=placed,
        out_specs=(P("rows", "feat"), P(None, "feat"), P(None, "feat")),
        check_vma=False,
    )
```

```python
import functools

import jax
import jax.numpy as jnp
from jax import lax
from jax.experimental import pallas as pl
from jax.experimental.pallas import tpu as pltpu
from jax.sharding import PartitionSpec as P

BF = jnp.bfloat16
F32 = jnp.float32
VMEM = pl.BlockSpec(memory_space=pltpu.VMEM)
SMEM = pl.BlockSpec(memory_space=pltpu.SMEM)
HBM = pl.BlockSpec(memory_space=pltpu.HBM)


def dot(a, b):
    return jnp.dot(a, b, preferred_element_type=F32)


def dot_nt(a, b):
    return lax.dot_general(a, b, (((1,), (1,)), ((), ())), preferred_element_type=F32)


def call(body, outs, specs, args, flops=0, scratch=(), limit=None):
    moved = sum(a.size * a.dtype.itemsize for a in args)
    moved += sum(o.size * o.dtype.itemsize for o in outs)
    return pl.pallas_call(
        body,
        out_shape=outs,
        in_specs=specs,
        out_specs=[VMEM] * len(outs),
        scratch_shapes=scratch,
        compiler_params=pltpu.CompilerParams(vmem_limit_bytes=limit or 32 * 1024 * 1024),
        cost_estimate=pl.CostEstimate(flops=flops, bytes_accessed=moved, transcendentals=0),
    )(*args)


def sds(shape, dtype):
    return jax.ShapeDtypeStruct(shape, dtype)


def assemble_kernel(all_counts, all_cols, vals, adj, counts, cols, tiles, acc, sems):
    nblocks = counts.shape[0]
    tile = vals.shape[1]
    pairs = ((all_counts, counts), (all_cols, cols), (vals, tiles))
    copies = [pltpu.make_async_copy(*pair, sems.at[i]) for i, pair in enumerate(pairs)]
    for copy in copies:
        copy.start()
    acc[...] = jnp.zeros_like(acc)
    for copy in copies:
        copy.wait()
    start = jnp.int32(0)
    for b in range(nblocks):
        rows = slice(b * tile, (b + 1) * tile)

        def add(t, carry, rows=rows):
            place = pl.ds(pl.multiple_of(cols[t] * tile, tile), tile)
            acc[rows, place] += tiles[t].astype(F32)
            return carry

        end = start + counts[b]
        lax.fori_loop(start, end, add, 0)
        start = end
    adj[...] = acc[...].astype(BF)


def flip_kernel(tile, adj, adj_t):
    def flip(c, carry):
        place = pl.ds(pl.multiple_of(c * tile, tile), tile)
        adj_t[place, :] = adj[:, place].T
        return carry

    lax.fori_loop(0, adj.shape[1] // tile, flip, 0)


def prepare_kernel(nf, feats, weight, root, mine, near, far, right):
    width = weight.shape[1]
    me = lax.axis_index("feat")
    mine[...] = feats[...]
    for k in range(nf // 2):
        place = slice(k * width, (k + 1) * width)
        for flip, out in ((0, near), (1, far)):
            rows = pl.ds(pl.multiple_of((me ^ (2 * k + flip)) * width, width), width)
            out[0, place, :] = weight[rows, :]
            out[1, place, :] = root[rows, :]
            into = slice((2 * k + flip) * width, (2 * k + flip + 1) * width)
            right[into, :] = jnp.concatenate([weight[rows, :], root[rows, :]], 1)


def forward_kernel(nf, *refs):
    pieces, (right, hidden, own) = refs[:nf], refs[nf:]
    rows, width = hidden.shape
    half = rows // 2
    for at in (0, half):
        part = slice(at, at + half)
        left = jnp.concatenate([piece[part, :] for piece in pieces], 1)
        total = dot(left, right[...])
        hidden[part, :] = total[:, :width].astype(BF)
        own[part, :] = total[:, width:]


def transpose_kernel(nf, *refs):
    pieces, out = refs[:nf], refs[nf]
    me = lax.axis_index("feat")
    width = pieces[0].shape[1]
    for m in range(nf):
        rows = pl.ds(pl.multiple_of((me ^ m) * width, width), width)
        out[rows, :] = pieces[m][...].T


def begin_kernel(adj, hidden, hidden_1, own, pre):
    rows = own.shape[0]
    me = lax.axis_index("rows")
    half = rows // 2
    for at in (0, half):
        part = slice(at, at + half)
        total = own[part, :]
        for j, block in enumerate((hidden, hidden_1)):
            place = pl.ds(pl.multiple_of((me ^ j) * rows, rows), rows)
            total = total + dot(adj[part, place], block[...])
        pre[part, :] = total


def aggregate_kernel(nr, *refs):
    hidden = refs[: nr - 2]
    adj, adj_t, begun, grad_out, grad_pre = refs[nr - 2 : nr + 3]
    sent = refs[nr + 3 :]
    me = lax.axis_index("rows")
    rows = begun.shape[0]
    places = [pl.ds(pl.multiple_of((me ^ j) * rows, rows), rows) for j in range(1, nr)]
    half = rows // 2
    for at in (0, half):
        part = slice(at, at + half)
        pre = begun[part, :]
        for j in range(1, nr - 1):
            pre = pre + dot(adj[part, places[j]], hidden[j - 1][...])
        sig = jax.nn.sigmoid(pre)
        grad = grad_out[part, :].astype(F32) * sig * (1.0 + pre * (1.0 - sig))
        grad_pre[part, :] = grad.astype(BF)
    for j in range(nr - 1):
        for at in (0, half):
            place = pl.ds(pl.multiple_of((me ^ (j + 1)) * rows + at, half), half)
            sent[j][at : at + half, :] = dot(adj_t[place, :], grad_pre[...]).astype(BF)


def keep_kernel(adj_t, grad_pre, kept):
    rows = kept.shape[0]
    place = pl.ds(pl.multiple_of(lax.axis_index("rows") * rows, rows), rows)
    kept[...] = dot(adj_t[place, :], grad_pre[...])


def sum_kernel(n, *refs):
    total = refs[0][...].astype(F32)
    for ref in refs[1:n]:
        total = total + ref[...].astype(F32)
    refs[n][...] = total.astype(refs[n].dtype)


def back_kernel(nz, near, near_2, back):
    width = near.shape[2]
    for k in range(nz):
        place = slice(k * width, (k + 1) * width)
        rows = [near[0, place, :], near[1, place, :], near_2[0, place, :], near_2[1, place, :]]
        back[:, place] = jnp.concatenate(rows, 1).T


def feats_kernel(nz, hidden, pre, hidden_2, pre_2, back, *out):
    rows, width = hidden.shape
    half = rows // 2
    for at in (0, half):
        part = slice(at, at + half)
        arrays = hidden, pre, hidden_2, pre_2
        total = dot(jnp.concatenate([array[part, :] for array in arrays], 1), back[...])
        for k in range(nz):
            out[k][part, :] = total[:, k * width : (k + 1) * width].astype(out[k].dtype)


def weights_kernel(feats_t, grads, top, bottom):
    half = top.shape[0]
    step = half // 2
    for at in range(0, 2 * half, step):
        out = top if at < half else bottom
        place = slice(at % half, at % half + step)
        out[place, :] = dot(feats_t[at : at + step, :], grads[...]).astype(BF)


def join_kernel(weight, root, root_2, out):
    width = weight.shape[1]
    out[:, :width] = weight[...]
    out[:, width:] = (root[...].astype(F32) + root_2[...].astype(F32)).astype(BF)


def pair_sum_kernel(top, top_2, bottom, bottom_2, top_sum, bottom_sum):
    for out, terms in ((top_sum, (top, top_2)), (bottom_sum, (bottom, bottom_2))):
        width = out.shape[1]
        total = terms[0][:, :width].astype(F32) + terms[1][:, :width].astype(F32)
        out[...] = total.astype(BF)


def place_kernel(top, top_2, bottom, bottom_2, out):
    half, width = top.shape[0], out.shape[1]
    for at, terms in ((0, (top, top_2)), (half, (bottom, bottom_2))):
        total = terms[0][...].astype(F32) + terms[1][...].astype(F32)
        out[at : at + half, :] = total[:, -width:]


def on_device(node_feats, weight, root_weight, grad_out, block_counts, tile_cols, tile_vals):
    rows, width = node_feats.shape
    depth = weight.shape[0]
    nr, nf = lax.axis_size("rows"), lax.axis_size("feat")
    nz = nf // 2
    nodes = rows * nr

    def swap(array, axis, mask):
        return lax.ppermute(array, axis, [(i, i ^ mask) for i in range(lax.axis_size(axis))])

    (adj,) = call(
        assemble_kernel,
        [sds((rows, nodes), BF)],
        [HBM] * 3,
        (block_counts, tile_cols, tile_vals),
        flops=4 * rows * nodes,
        scratch=[
            pltpu.SMEM(block_counts.shape, jnp.int32),
            pltpu.SMEM(tile_cols.shape, jnp.int32),
            pltpu.VMEM(tile_vals.shape, BF),
            pltpu.VMEM((rows, nodes), F32),
            pltpu.SemaphoreType.DMA((3,)),
        ],
        limit=48 * 1024 * 1024,
    )
    mine, near, far, right = call(
        functools.partial(prepare_kernel, nf),
        [sds((rows, width), BF)]
        + [sds((2, depth // 2, width), BF)] * 2
        + [sds((depth, 2 * width), BF)],
        [VMEM] * 3,
        (node_feats, weight, root_weight),
    )
    (adj_t,) = call(
        functools.partial(flip_kernel, tile_vals.shape[1]), [sds((nodes, rows), BF)], [VMEM], (adj,)
    )
    ranks = sorted(range(1, nz), key=lambda k: (k < nz // 2, k))
    masks = [1 << bit for bit in range(1, nf.bit_length() - 1)]
    moved = {0: node_feats}
    for mask in reversed(masks[1:]):
        moved |= {m | mask: swap(piece, "feat", mask) for m, piece in moved.items()}
    moved[masks[0]] = swap(node_feats, "feat", masks[0])
    beside = {0: swap(node_feats, "feat", 1)}
    order = sorted((m for m in moved if m), reverse=True)
    *early, near, beside[0] = lax.optimization_barrier((*[moved[m] for m in order], near, beside[0]))
    moved |= dict(zip(order, early))
    ahead = {m: swap(moved[m], "feat", 1) for m in order}
    last = [m | masks[0] for m in order if m != masks[0]]
    moved |= {m: swap(moved[m ^ masks[0]], "feat", masks[0]) for m in last}
    held = lax.optimization_barrier((*[moved[m] for m in last], *[ahead[m] for m in order]))
    moved |= dict(zip(last, held))
    beside |= dict(zip(order, held[len(last) :]))
    beside |= {m: swap(moved[m], "feat", 1) for m in last}
    moved[0] = mine
    pieces = [piece for m in sorted(moved) for piece in (moved[m], beside[m])]
    near_2 = swap(far, "feat", 1)
    hidden, own = call(
        functools.partial(forward_kernel, nf),
        [sds((rows, width), BF), sds((rows, width), F32)],
        [VMEM] * (nf + 1),
        (*pieces, right),
        flops=4 * rows * depth * width,
    )
    gathered = [hidden] + [swap(hidden, "rows", j) for j in range(1, nr)]
    (feats_t,) = call(
        functools.partial(transpose_kernel, nf),
        [sds((depth, rows), BF)],
        [VMEM] * nf,
        pieces,
    )
    (back,) = call(
        functools.partial(back_kernel, nz),
        [sds((4 * width, depth // 2), BF)],
        [VMEM] * 2,
        (near, near_2),
    )
    adj_t, back, feats_t = lax.optimization_barrier((adj_t, back, feats_t))
    (begun,) = call(
        begin_kernel,
        [sds((rows, width), F32)],
        [VMEM] * 4,
        (adj, hidden, gathered[1], own),
        flops=2 * rows * rows * width,
    )
    grad_pre, *sent = call(
        functools.partial(aggregate_kernel, nr),
        [sds((rows, width), BF)] * nr,
        [VMEM] * (nr + 2),
        (*gathered[2:], adj, adj_t, begun, grad_out),
        flops=4 * rows * nodes * width,
        limit=max(32 * 1024 * 1024, 10 * rows * nodes),
    )
    root_part = call(
        weights_kernel,
        [sds((depth // 2, width), BF)] * 2,
        [VMEM] * 2,
        (feats_t, grad_pre),
        flops=2 * rows * depth * width,
    )
    (kept,) = call(
        keep_kernel,
        [sds((rows, width), F32)],
        [VMEM] * 2,
        (adj_t, grad_pre),
        flops=2 * rows * rows * width,
    )
    pre_2 = swap(grad_pre, "feat", 1)
    sums = [kept] + [swap(part, "rows", j + 1) for j, part in enumerate(sent)]
    (grad_hidden,) = call(
        functools.partial(sum_kernel, nr), [sds((rows, width), BF)], [VMEM] * nr, sums
    )
    hidden_2 = swap(grad_hidden, "feat", 1)
    parts = call(
        functools.partial(feats_kernel, nz),
        [sds((rows, width), BF if k else F32) for k in range(nz)],
        [VMEM] * 5,
        (grad_hidden, grad_pre, hidden_2, pre_2, back),
        flops=4 * rows * depth * width,
    )
    weight_part = call(
        weights_kernel,
        [sds((depth // 2, width), BF)] * 2,
        [VMEM] * 2,
        (feats_t, grad_hidden),
        flops=2 * rows * depth * width,
    )
    steps = [1 << bit for bit in range(nr.bit_length() - 1)]
    first, *between = zip(reversed(steps), steps)
    final = between[-1]
    root_got = [swap(part, "rows", mask) for part, mask in zip(root_part, first)]
    sums_f = [parts[0]] + [swap(parts[k], "feat", 2 * k) for k in ranks]
    joined = [sds((depth // 2, 2 * width), BF)] * 2
    grads = [
        call(join_kernel, joined[:1], [VMEM] * 3, arrays)[0]
        for arrays in zip(weight_part, root_part, root_got)
    ]
    for masks in between:
        got = [swap(part, "rows", mask) for part, mask in zip(grads, masks)]
        pairs = grads[0], got[0], grads[1], got[1]
        last = masks == final
        shapes = [sds((depth // 2, width), BF)] * 2 if last else joined
        grads = call(pair_sum_kernel, shapes, [VMEM] * 4, pairs)

    def place(top, top_2, bottom, bottom_2):
        arrays = top, top_2, bottom, bottom_2
        return call(place_kernel, [sds((depth, width), F32)], [VMEM] * 4, arrays)[0]

    def finish(operands):
        grads, pairs = operands
        got = [swap(part, "rows", mask) for part, mask in zip(grads, first)]
        return place(grads[0], got[0], grads[1], got[1]), place(*pairs)

    def skip(operands):
        return (jnp.zeros((depth, width), F32),) * 2

    operands = tuple(grads), tuple(pairs)
    grad_weight, grad_root = lax.cond(block_counts[0] > 0, finish, skip, operands)
    *sums_f, grad_weight, grad_root = lax.optimization_barrier((*sums_f, grad_weight, grad_root))
    (grad_feats,) = call(
        functools.partial(sum_kernel, len(sums_f)),
        [sds((rows, width), BF)],
        [VMEM] * len(sums_f),
        sums_f,
    )
    return grad_feats, grad_weight, grad_root


def solution(mesh):
    placed = (
        P("rows", "feat"),
        P(None, "feat"),
        P(None, "feat"),
        P("rows", "feat"),
        P("rows"),
        P("rows"),
        P("rows", None, None),
    )
    return jax.shard_map(
        on_device,
        mesh=mesh,
        in_specs=placed,
        out_specs=(P("rows", "feat"), P(None, "feat"), P(None, "feat")),
        check_vma=False,
    )
```

```python
import functools

import jax
import jax.numpy as jnp
from jax import lax
from jax.experimental import pallas as pl
from jax.experimental.pallas import tpu as pltpu
from jax.sharding import PartitionSpec as P

BF = jnp.bfloat16
F32 = jnp.float32
VMEM = pl.BlockSpec(memory_space=pltpu.VMEM)
SMEM = pl.BlockSpec(memory_space=pltpu.SMEM)
HBM = pl.BlockSpec(memory_space=pltpu.HBM)


def dot(a, b):
    return jnp.dot(a, b, preferred_element_type=F32)


def dot_nt(a, b):
    return lax.dot_general(a, b, (((1,), (1,)), ((), ())), preferred_element_type=F32)


def call(body, outs, specs, args, flops=0, scratch=(), limit=None):
    moved = sum(a.size * a.dtype.itemsize for a in args)
    moved += sum(o.size * o.dtype.itemsize for o in outs)
    return pl.pallas_call(
        body,
        out_shape=outs,
        in_specs=specs,
        out_specs=[VMEM] * len(outs),
        scratch_shapes=scratch,
        compiler_params=pltpu.CompilerParams(vmem_limit_bytes=limit or 32 * 1024 * 1024),
        cost_estimate=pl.CostEstimate(flops=flops, bytes_accessed=moved, transcendentals=0),
    )(*args)


def sds(shape, dtype):
    return jax.ShapeDtypeStruct(shape, dtype)


def assemble_kernel(all_counts, all_cols, vals, adj, counts, cols, tiles, acc, sems):
    nblocks = counts.shape[0]
    tile = vals.shape[1]
    pairs = ((all_counts, counts), (all_cols, cols), (vals, tiles))
    copies = [pltpu.make_async_copy(*pair, sems.at[i]) for i, pair in enumerate(pairs)]
    for copy in copies:
        copy.start()
    acc[...] = jnp.zeros_like(acc)
    for copy in copies:
        copy.wait()
    start = jnp.int32(0)
    for b in range(nblocks):
        rows = slice(b * tile, (b + 1) * tile)

        def add(t, carry, rows=rows):
            place = pl.ds(pl.multiple_of(cols[t] * tile, tile), tile)
            acc[rows, place] += tiles[t].astype(F32)
            return carry

        end = start + counts[b]
        lax.fori_loop(start, end, add, 0)
        start = end
    adj[...] = acc[...].astype(BF)


def flip_kernel(tile, adj, adj_t):
    def flip(c, carry):
        place = pl.ds(pl.multiple_of(c * tile, tile), tile)
        adj_t[place, :] = adj[:, place].T
        return carry

    lax.fori_loop(0, adj.shape[1] // tile, flip, 0)


def prepare_kernel(nf, feats, weight, root, mine, near, far, right):
    width = weight.shape[1]
    me = lax.axis_index("feat")
    mine[...] = feats[...]
    for k in range(nf // 2):
        place = slice(k * width, (k + 1) * width)
        for flip, out in ((0, near), (1, far)):
            rows = pl.ds(pl.multiple_of((me ^ (2 * k + flip)) * width, width), width)
            out[0, place, :] = weight[rows, :]
            out[1, place, :] = root[rows, :]
            into = slice((2 * k + flip) * width, (2 * k + flip + 1) * width)
            right[into, :] = jnp.concatenate([weight[rows, :], root[rows, :]], 1)


def forward_kernel(nf, *refs):
    pieces, (right, hidden, own) = refs[:nf], refs[nf:]
    rows, width = hidden.shape
    step = rows // 2
    for at in range(0, rows, step):
        part = slice(at, at + step)
        total = None
        for k in range(0, nf, 2):
            left = jnp.concatenate([pieces[k][part, :], pieces[k + 1][part, :]], 1)
            product = dot(left, right[k * width : (k + 2) * width, :])
            total = product if total is None else total + product
        hidden[part, :] = total[:, :width].astype(BF)
        own[part, :] = total[:, width:]


def transpose_kernel(nf, *refs):
    pieces, out = refs[:nf], refs[nf]
    me = lax.axis_index("feat")
    width = pieces[0].shape[1]
    for m in range(nf):
        rows = pl.ds(pl.multiple_of((me ^ m) * width, width), width)
        out[rows, :] = pieces[m][...].T


def begin_kernel(adj, hidden, hidden_1, own, pre):
    rows = own.shape[0]
    me = lax.axis_index("rows")
    half = rows // 2
    for at in (0, half):
        part = slice(at, at + half)
        total = own[part, :]
        for j, block in enumerate((hidden, hidden_1)):
            place = pl.ds(pl.multiple_of((me ^ j) * rows, rows), rows)
            total = total + dot(adj[part, place], block[...])
        pre[part, :] = total


def aggregate_kernel(nr, *refs):
    hidden = refs[: nr - 2]
    adj, adj_t, begun, grad_out, grad_pre = refs[nr - 2 : nr + 3]
    sent = refs[nr + 3 :]
    me = lax.axis_index("rows")
    rows = begun.shape[0]
    places = [pl.ds(pl.multiple_of((me ^ j) * rows, rows), rows) for j in range(1, nr)]
    half = rows // 2
    for at in (0, half):
        part = slice(at, at + half)
        pre = begun[part, :]
        for j in range(1, nr - 1):
            pre = pre + dot(adj[part, places[j]], hidden[j - 1][...])
        sig = jax.nn.sigmoid(pre)
        grad = grad_out[part, :].astype(F32) * sig * (1.0 + pre * (1.0 - sig))
        grad_pre[part, :] = grad.astype(BF)
    for j in range(nr - 1):
        for at in (0, half):
            place = pl.ds(pl.multiple_of((me ^ (j + 1)) * rows + at, half), half)
            sent[j][at : at + half, :] = dot(adj_t[place, :], grad_pre[...]).astype(BF)


def keep_kernel(adj_t, grad_pre, kept):
    rows = kept.shape[0]
    place = pl.ds(pl.multiple_of(lax.axis_index("rows") * rows, rows), rows)
    kept[...] = dot(adj_t[place, :], grad_pre[...])


def sum_kernel(n, *refs):
    total = refs[0][...].astype(F32)
    for ref in refs[1:n]:
        total = total + ref[...].astype(F32)
    refs[n][...] = total.astype(refs[n].dtype)


def back_kernel(nz, near, near_2, back):
    width = near.shape[2]
    for k in range(nz):
        place = slice(k * width, (k + 1) * width)
        rows = [near[0, place, :], near[1, place, :], near_2[0, place, :], near_2[1, place, :]]
        back[:, place] = jnp.concatenate(rows, 1).T


def feats_kernel(nz, hidden, pre, hidden_2, pre_2, back, *out):
    rows, width = hidden.shape
    half = rows // 2
    for at in (0, half):
        part = slice(at, at + half)
        arrays = hidden, pre, hidden_2, pre_2
        total = dot(jnp.concatenate([array[part, :] for array in arrays], 1), back[...])
        for k in range(nz):
            out[k][part, :] = total[:, k * width : (k + 1) * width].astype(out[k].dtype)


def weights_kernel(feats_t, grads, top, bottom):
    half = top.shape[0]
    step = half // 2
    for at in range(0, 2 * half, step):
        out = top if at < half else bottom
        place = slice(at % half, at % half + step)
        out[place, :] = dot(feats_t[at : at + step, :], grads[...]).astype(BF)


def join_kernel(weight, root, root_2, out):
    width = weight.shape[1]
    out[:, :width] = weight[...]
    out[:, width:] = (root[...].astype(F32) + root_2[...].astype(F32)).astype(BF)


def pair_sum_kernel(top, top_2, bottom, bottom_2, top_sum, bottom_sum):
    for out, terms in ((top_sum, (top, top_2)), (bottom_sum, (bottom, bottom_2))):
        width = out.shape[1]
        total = terms[0][:, :width].astype(F32) + terms[1][:, :width].astype(F32)
        out[...] = total.astype(BF)


def place_kernel(top, top_2, bottom, bottom_2, out):
    half, width = top.shape[0], out.shape[1]
    for at, terms in ((0, (top, top_2)), (half, (bottom, bottom_2))):
        total = terms[0][...].astype(F32) + terms[1][...].astype(F32)
        out[at : at + half, :] = total[:, -width:]


def on_device(node_feats, weight, root_weight, grad_out, block_counts, tile_cols, tile_vals):
    rows, width = node_feats.shape
    depth = weight.shape[0]
    nr, nf = lax.axis_size("rows"), lax.axis_size("feat")
    nz = nf // 2
    nodes = rows * nr

    def swap(array, axis, mask):
        return lax.ppermute(array, axis, [(i, i ^ mask) for i in range(lax.axis_size(axis))])

    (adj,) = call(
        assemble_kernel,
        [sds((rows, nodes), BF)],
        [HBM] * 3,
        (block_counts, tile_cols, tile_vals),
        flops=4 * rows * nodes,
        scratch=[
            pltpu.SMEM(block_counts.shape, jnp.int32),
            pltpu.SMEM(tile_cols.shape, jnp.int32),
            pltpu.VMEM(tile_vals.shape, BF),
            pltpu.VMEM((rows, nodes), F32),
            pltpu.SemaphoreType.DMA((3,)),
        ],
        limit=48 * 1024 * 1024,
    )
    mine, near, far, right = call(
        functools.partial(prepare_kernel, nf),
        [sds((rows, width), BF)]
        + [sds((2, depth // 2, width), BF)] * 2
        + [sds((depth, 2 * width), BF)],
        [VMEM] * 3,
        (node_feats, weight, root_weight),
    )
    (adj_t,) = call(
        functools.partial(flip_kernel, tile_vals.shape[1]), [sds((nodes, rows), BF)], [VMEM], (adj,)
    )
    ranks = sorted(range(1, nz), key=lambda k: (k < nz // 2, k))
    masks = [1 << bit for bit in range(1, nf.bit_length() - 1)]
    moved = {0: node_feats}
    for mask in reversed(masks[1:]):
        moved |= {m | mask: swap(piece, "feat", mask) for m, piece in moved.items()}
    moved[masks[0]] = swap(node_feats, "feat", masks[0])
    beside = {0: swap(node_feats, "feat", 1)}
    order = sorted((m for m in moved if m), reverse=True)
    *early, near, beside[0] = lax.optimization_barrier((*[moved[m] for m in order], near, beside[0]))
    moved |= dict(zip(order, early))
    ahead = {m: swap(moved[m], "feat", 1) for m in order}
    last = [m | masks[0] for m in order if m != masks[0]]
    moved |= {m: swap(moved[m ^ masks[0]], "feat", masks[0]) for m in last}
    held = lax.optimization_barrier((*[moved[m] for m in last], *[ahead[m] for m in order]))
    moved |= dict(zip(last, held))
    beside |= dict(zip(order, held[len(last) :]))
    beside |= {m: swap(moved[m], "feat", 1) for m in last}
    moved[0] = mine
    pieces = [piece for m in sorted(moved) for piece in (moved[m], beside[m])]
    near_2 = swap(far, "feat", 1)
    hidden, own = call(
        functools.partial(forward_kernel, nf),
        [sds((rows, width), BF), sds((rows, width), F32)],
        [VMEM] * (nf + 1),
        (*pieces, right),
        flops=4 * rows * depth * width,
    )
    gathered = [hidden] + [swap(hidden, "rows", j) for j in range(1, nr)]
    (feats_t,) = call(
        functools.partial(transpose_kernel, nf),
        [sds((depth, rows), BF)],
        [VMEM] * nf,
        pieces,
    )
    (back,) = call(
        functools.partial(back_kernel, nz),
        [sds((4 * width, depth // 2), BF)],
        [VMEM] * 2,
        (near, near_2),
    )
    adj_t, back, feats_t = lax.optimization_barrier((adj_t, back, feats_t))
    (begun,) = call(
        begin_kernel,
        [sds((rows, width), F32)],
        [VMEM] * 4,
        (adj, hidden, gathered[1], own),
        flops=2 * rows * rows * width,
    )
    grad_pre, *sent = call(
        functools.partial(aggregate_kernel, nr),
        [sds((rows, width), BF)] * nr,
        [VMEM] * (nr + 2),
        (*gathered[2:], adj, adj_t, begun, grad_out),
        flops=4 * rows * nodes * width,
        limit=max(32 * 1024 * 1024, 10 * rows * nodes),
    )
    root_part = call(
        weights_kernel,
        [sds((depth // 2, width), BF)] * 2,
        [VMEM] * 2,
        (feats_t, grad_pre),
        flops=2 * rows * depth * width,
    )
    (kept,) = call(
        keep_kernel,
        [sds((rows, width), F32)],
        [VMEM] * 2,
        (adj_t, grad_pre),
        flops=2 * rows * rows * width,
    )
    pre_2 = swap(grad_pre, "feat", 1)
    sums = [kept] + [swap(part, "rows", j + 1) for j, part in enumerate(sent)]
    (grad_hidden,) = call(
        functools.partial(sum_kernel, nr), [sds((rows, width), BF)], [VMEM] * nr, sums
    )
    hidden_2 = swap(grad_hidden, "feat", 1)
    parts = call(
        functools.partial(feats_kernel, nz),
        [sds((rows, width), BF if k else F32) for k in range(nz)],
        [VMEM] * 5,
        (grad_hidden, grad_pre, hidden_2, pre_2, back),
        flops=4 * rows * depth * width,
    )
    weight_part = call(
        weights_kernel,
        [sds((depth // 2, width), BF)] * 2,
        [VMEM] * 2,
        (feats_t, grad_hidden),
        flops=2 * rows * depth * width,
    )
    steps = [1 << bit for bit in range(nr.bit_length() - 1)]
    first, *between = zip(reversed(steps), steps)
    final = between[-1]
    root_got = [swap(part, "rows", mask) for part, mask in zip(root_part, first)]
    sums_f = [parts[0]] + [swap(parts[k], "feat", 2 * k) for k in ranks]
    joined = [sds((depth // 2, 2 * width), BF)] * 2
    grads = [
        call(join_kernel, joined[:1], [VMEM] * 3, arrays)[0]
        for arrays in zip(weight_part, root_part, root_got)
    ]
    for masks in between[:-1]:
        got = [swap(part, "rows", mask) for part, mask in zip(grads, masks)]
        grads = call(pair_sum_kernel, joined, [VMEM] * 4, (grads[0], got[0], grads[1], got[1]))
    got = [swap(part, "rows", mask) for part, mask in zip(grads, final)]
    pairs = grads[0], got[0], grads[1], got[1]

    def place(top, top_2, bottom, bottom_2):
        arrays = top, top_2, bottom, bottom_2
        return call(place_kernel, [sds((depth, width), F32)], [VMEM] * 4, arrays)[0]

    def finish(operands):
        pairs = operands
        shapes = [sds((depth // 2, width), BF)] * 2
        grads = call(pair_sum_kernel, shapes, [VMEM] * 4, pairs)
        got = [swap(part, "rows", mask) for part, mask in zip(grads, first)]
        return place(grads[0], got[0], grads[1], got[1]), place(*pairs)

    def skip(operands):
        return (jnp.zeros((depth, width), F32),) * 2

    operands = tuple(pairs)
    grad_weight, grad_root = lax.cond(block_counts[0] > 0, finish, skip, operands)
    *sums_f, grad_weight, grad_root = lax.optimization_barrier((*sums_f, grad_weight, grad_root))
    (grad_feats,) = call(
        functools.partial(sum_kernel, len(sums_f)),
        [sds((rows, width), BF)],
        [VMEM] * len(sums_f),
        sums_f,
    )
    return grad_feats, grad_weight, grad_root


def solution(mesh):
    placed = (
        P("rows", "feat"),
        P(None, "feat"),
        P(None, "feat"),
        P("rows", "feat"),
        P("rows"),
        P("rows"),
        P("rows", None, None),
    )
    return jax.shard_map(
        on_device,
        mesh=mesh,
        in_specs=placed,
        out_specs=(P("rows", "feat"), P(None, "feat"), P(None, "feat")),
        check_vma=False,
    )
```
